512 devices in a mesh: segment: 2 (over core), rows: 128 (over z, y_lo, x), mp: 2 (over y_hi).
Axes of the slice: x: 4, y: 8 (y_hi: 2, y_lo: 4; y = y_hi * 4 + y_lo), z: 8, core: 2. Of those that a mesh axis runs over, the one named last changes fastest.
Arguments:
- start_state: bfloat16 [8192, 2048], P('rows', 'mp'), may hold values from -6 to 6
- expert_ids: int32 [3, 8192, 8], P(None, 'rows'), may hold values from 0 to 127, all different within a row; in each aligned block of 64 rows (0 to 63, 64 to 127, ..., all dimensions but the last counted through in order) at most 8 rows name the same one
- norm_gain: float32 [2048], P('mp'), may hold values from 0.1 to 1.9
- w_router: bfloat16 [2048, 128], P('mp'), may hold values from -0.125 to 0.125
- w_gate: bfloat16 [128, 2048, 384], P('rows', None, 'mp'), may hold values from -0.125 to 0.125
- w_up: bfloat16 [128, 2048, 384], P('rows', None, 'mp'), may hold values from -0.125 to 0.125
- w_down: bfloat16 [128, 384, 2048], P('rows', 'mp'), may hold values from -0.3125 to 0.3125
- w_in: bfloat16 [2048, 1024], P(None, 'mp'), may hold values from -0.125 to 0.125
- trans_taps: float32 [4, 1024], P(None, 'mp'), may hold values from -4 to 4
- dw_kernels: float32 [2, 7, 1024], P(None, None, 'mp'), may hold values from -2.5 to 2.5
- ln_gain: float32 [2, 1024], P(None, 'mp'), may hold values from 0.1 to 1.9
- ln_bias: float32 [2, 1024], P(None, 'mp'), may hold values from -3 to 3
- w_out: float32 [1024], P('mp'), may hold values from -0.1875 to 0.1875
Outputs:
- talker_state: bfloat16 [8192, 2048], P('rows', 'mp')
- audio: float32 [2, 3, 16384], P('segment', None, 'rows')
The draws below stay inside these ranges and needn't reach their ends.
Inputs may be any that keep to these rules, and one draw needn't show every extreme that they name: `expert_ids`: each frame names 8 different experts. In each pass no expert is named by more than 8 rows of one aligned block of 64 rows, and in some blocks one is named by exactly 8.
All inputs are finite; a program needn't handle non-finite values.
Results may differ from the reference program's by a relative error of at most 0.014.
Values may be sent and summed in bfloat16 or wider, within the bound.
No kernel may reach another device: no remote copies, remote signals or barrier semaphores. Data moves between devices by JAX's collectives and lax.ppermute only.
A program may use at most 64 MiB of HBM per device.

```python
import math
import jax
import jax.numpy as jnp
import numpy as np
from jax import lax

D = 2048
TOPK = 8
E = 128
FFW = 384
C = 1024
KW = 7
VL = 2
STEPS = 3
ROWS_DEV = 64
CAP = 8
BEAMS = 8192
TIME = 16384
N_ROWS = 128
N_MP = 2


def steps_of(key, extent, pieces, low, high):
    factor_of, own = 1.0, jax.random.fold_in(key, 6)
    for axis_at, shards_of in pieces:
        steps = jnp.exp(jax.random.uniform(jax.random.fold_in(own, axis_at), (shards_of,), jnp.float32, low / len(pieces), high / len(pieces)))
        factor_of = factor_of * jnp.repeat(steps, extent[axis_at] // shards_of).reshape([-1 if axis == axis_at else 1 for axis in range(len(extent))])
    return factor_of


def routed_block(own_key, own, number, rows, count, top, most, lean):
    order = jax.random.permutation(own_key, count)
    packed, usual = shares(count, rows * top, most, lean, True), shares(count, rows * top, most, lean, False)
    places = jnp.arange(count)

    def named(lengths, rotation):
        used = int((lengths > 0).sum())
        fixed = max(1, used // 4)
        passed = fixed + (places - fixed + rotation * (used - fixed)) % max(1, count - fixed)
        return jnp.zeros((count,), jnp.int32).at[order[jnp.where(places < fixed, places, passed)]].set(jnp.asarray(lengths, jnp.int32))

    lengths = jnp.where(number % 4 == 0, named(packed, number // 4), named(usual, number - number // 4 - 1))
    mixed = jax.random.permutation(jax.random.fold_in(own, 3), count)
    giver, sink = mixed[0:count // 2 * 2:2], mixed[1:count // 2 * 2:2]
    room = jnp.minimum(lengths[giver] - 1, most - lengths[sink]) // 2
    room = jnp.where((giver == order[0]) | (sink == order[0]) | (lengths[sink] == 0), 0, jnp.maximum(room, 0))
    passed = jax.random.randint(jax.random.fold_in(own, 4), (count // 2,), 0, 1 << 20) % (room + 1)
    lengths = lengths.at[giver].add(-passed).at[sink].add(passed)
    labels = jnp.searchsorted(jnp.cumsum(lengths), jnp.arange(rows * top), side="right").astype(jnp.int32)
    table = labels.reshape(top, rows).T
    table = table[jax.random.permutation(jax.random.fold_in(own, 1), rows)]
    rotation = jax.random.randint(jax.random.fold_in(own, 2), (rows, 1), 0, top)
    return jnp.take_along_axis(table, (jnp.arange(top)[None, :] + rotation) % top, axis=1)


def shares(amount, total, limit, lean, full):
    weights = [(1 << 20) // math.isqrt(rank ** lean) + 1 for rank in range(1, amount + 1)]
    largest = limit if full else min(limit, max(-(-total // amount), total * weights[0] // sum(weights)))
    least = 1 if total - largest >= amount - 1 else 0
    holding, spare = [largest] + [least] * (amount - 1), total - largest - least * (amount - 1)
    while spare > 0:
        free = [i for i in range(1, amount) if holding[i] < largest] or [i for i in range(1, amount) if holding[i] < limit]
        whole, remaining = sum([weights[i] for i in free]), spare
        for i in free:
            addition = min(limit - holding[i], max(1, remaining * weights[i] // whole), spare)
            holding[i] = holding[i] + addition
            spare = spare - addition
    return np.array(holding)


def centred(own_key, shape, scale, most, shards=(), kind=jnp.bfloat16):
    factor_of = steps_of(own_key, shape, shards, -0.22, 0.18) if shards else 1.0
    drawn = jax.random.normal(own_key, shape, jnp.float32) * scale * factor_of
    return jnp.minimum(jnp.maximum(drawn, -most), most).astype(kind)


def setup_inputs(seed: int = 0) -> dict:
    arg_keys = jax.random.split(jax.random.key(seed), 14)
    start_state = centred(arg_keys[0], (BEAMS, D), 1.0, 6.0, ((0, 128), (1, 2)))
    expert_ids_keys = jax.random.split(jax.random.fold_in(arg_keys[1], 1), STEPS * BEAMS // ROWS_DEV)
    expert_ids_turns = jax.random.permutation(jax.random.fold_in(arg_keys[1], 3), STEPS * BEAMS // ROWS_DEV)
    expert_ids = jax.vmap(lambda own, number: routed_block(jax.random.fold_in(arg_keys[1], 2), own, number, ROWS_DEV, E, TOPK, CAP, 2))(expert_ids_keys, expert_ids_turns).reshape((STEPS, BEAMS, TOPK))
    norm_gain = jnp.clip(1.0 + 0.18 * jax.random.normal(arg_keys[2], (D,), jnp.float32), 0.1, 1.9)
    w_router = centred(arg_keys[3], (D, E), D ** -0.5, 0.125, ((0, 2),))
    w_gate = centred(arg_keys[4], (E, D, FFW), D ** -0.5, 0.125, ((0, 128), (2, 2)))
    w_up = centred(arg_keys[5], (E, D, FFW), D ** -0.5, 0.125, ((0, 128), (2, 2)))
    w_down = centred(arg_keys[6], (E, FFW, D), FFW ** -0.5, 0.3125, ((0, 128), (1, 2)))
    w_in = centred(arg_keys[7], (D, C), D ** -0.5, 0.125, ((1, 2),))
    trans_taps = centred(arg_keys[8], (4, C), 0.7, 4.0, ((1, 2),), jnp.float32)
    dw_kernels = centred(arg_keys[9], (VL, KW, C), 0.4, 2.5, ((2, 2),), jnp.float32)
    ln_gain = jnp.clip(1.0 + 0.18 * jax.random.normal(arg_keys[10], (VL, C), jnp.float32), 0.1, 1.9)
    ln_bias = centred(arg_keys[11], (VL, C), 0.5, 3.0, ((1, 2),), jnp.float32)
    w_out = centred(arg_keys[12], (C,), C ** -0.5, 0.1875, ((0, 2),), jnp.float32)
    return dict(start_state=start_state, expert_ids=expert_ids, norm_gain=norm_gain, w_router=w_router, w_gate=w_gate, w_up=w_up, w_down=w_down, w_in=w_in, trans_taps=trans_taps, dw_kernels=dw_kernels, ln_gain=ln_gain, ln_bias=ln_bias, w_out=w_out)


def expert_apply(operands):
    slot_rows, gate_proj, up_proj, down_proj = operands
    gate_val = jnp.dot(slot_rows, gate_proj, preferred_element_type=jnp.float32)
    up_val = jnp.dot(slot_rows, up_proj, preferred_element_type=jnp.float32)
    active = (jax.nn.silu(gate_val) * up_val).astype(jnp.bfloat16)
    block_width = FFW // N_MP
    total = jnp.zeros((slot_rows.shape[0], D), jnp.float32)
    for block_index in range(N_MP):
        lower = block_index * block_width
        piece = jnp.dot(active[:, lower:lower + block_width], down_proj[lower:lower + block_width], preferred_element_type=jnp.float32).astype(jnp.bfloat16)
        total = total + piece.astype(jnp.float32)
    return total.astype(jnp.bfloat16)

def talker_step(hidden, step_ids, norm_gain, w_router, w_gate, w_up, w_down):
    hidden_f = hidden.astype(jnp.float32)
    mean_square = lax.optimization_barrier(jnp.mean(hidden_f * hidden_f, axis=1, keepdims=True))
    normed = (hidden_f * lax.rsqrt(mean_square + 1e-06) * norm_gain).astype(jnp.bfloat16)
    logits = jnp.dot(normed, w_router, preferred_element_type=jnp.float32)
    chosen = jnp.take_along_axis(logits, step_ids, axis=1)
    squashed = jax.nn.sigmoid(chosen)
    weights = squashed / lax.optimization_barrier(jnp.sum(squashed, axis=1, keepdims=True))
    block_ids = step_ids.reshape(N_ROWS, ROWS_DEV * TOPK)
    one_hot = (block_ids[:, :, None] == jnp.arange(E, dtype=jnp.int32)[None, None, :]).astype(jnp.int32)
    earlier = jnp.cumsum(one_hot, axis=1) - one_hot
    position = lax.optimization_barrier(jnp.sum(earlier * one_hot, axis=2))
    source = jnp.arange(N_ROWS, dtype=jnp.int32)[:, None]
    slot_index = (source * CAP + position).reshape(-1).astype(jnp.int32)
    expert_index = block_ids.reshape(-1).astype(jnp.int32)
    pair_rows = jnp.arange(ROWS_DEV * TOPK, dtype=jnp.int32)[None, :] // TOPK
    row_index = (source * ROWS_DEV + pair_rows).reshape(-1).astype(jnp.int32)
    buffer = jnp.zeros((E, N_ROWS * CAP, D), jnp.bfloat16)
    buffer = buffer.at[expert_index, slot_index].set(normed[row_index])
    results = lax.map(expert_apply, (buffer, w_gate, w_up, w_down))
    picked = results[expert_index, slot_index].astype(jnp.float32).reshape(BEAMS, TOPK, D)
    mixed = lax.optimization_barrier(jnp.sum(weights[:, :, None] * picked, axis=1))
    return (hidden_f + mixed).astype(jnp.bfloat16)

def vocoder(frames, w_in, trans_taps, dw_kernels, ln_gain, ln_bias, w_out):
    projected = jnp.dot(frames, w_in, preferred_element_type=jnp.float32).astype(jnp.bfloat16)
    current = projected.astype(jnp.float32)
    earlier = jnp.concatenate([jnp.zeros((1, C), jnp.float32), current[:-1]], axis=0)
    even_rows = trans_taps[0] * current + trans_taps[2] * earlier
    odd_rows = trans_taps[1] * current + trans_taps[3] * earlier
    signal = jnp.stack([even_rows, odd_rows], axis=1).reshape(TIME, C).astype(jnp.bfloat16)
    for layer_index in range(VL):
        dilation = 3 ** layer_index
        reach = (KW - 1) * dilation
        padded = jnp.concatenate([jnp.zeros((reach, C), jnp.float32), signal.astype(jnp.float32)], axis=0)
        mixed = jnp.zeros((TIME, C), jnp.float32)
        for tap_index in range(KW):
            start_row = reach - tap_index * dilation
            mixed = mixed + dw_kernels[layer_index, tap_index] * padded[start_row:start_row + TIME]
        center = lax.optimization_barrier(jnp.mean(mixed, axis=1, keepdims=True))
        spread = lax.optimization_barrier(jnp.mean(mixed * mixed, axis=1, keepdims=True)) - center * center
        normed = (mixed - center) * lax.rsqrt(spread + 1e-06)
        signal = (signal.astype(jnp.float32) + normed * ln_gain[layer_index] + ln_bias[layer_index]).astype(jnp.bfloat16)
    return lax.optimization_barrier(jnp.sum(signal.astype(jnp.float32) * w_out, axis=1))

def reference(start_state, expert_ids, norm_gain, w_router, w_gate, w_up, w_down, w_in, trans_taps, dw_kernels, ln_gain, ln_bias, w_out):
    hidden = start_state
    samples = []
    for tick_index in range(STEPS):
        hidden = talker_step(hidden, expert_ids[tick_index], norm_gain, w_router, w_gate, w_up, w_down)
        samples.append(vocoder(hidden, w_in, trans_taps, dw_kernels, ln_gain, ln_bias, w_out))
    sound = jnp.stack(samples, axis=0)
    return (hidden, jnp.stack([jnp.zeros_like(sound), sound], axis=0))
```

```python
import jax
import jax.numpy as jnp
from jax import lax
from jax.sharding import PartitionSpec as P

BF16 = jnp.bfloat16
F32 = jnp.float32


def swapped(block, axis):
    return lax.ppermute(block, axis, [(0, 1), (1, 0)])


def passed_along(block):
    count = lax.axis_size("rows")
    return lax.ppermute(block, "rows", [(i, i + 1) for i in range(count - 1)])


def dot(a, b):
    return jnp.dot(a, b, preferred_element_type=F32)


def other_half(weight, axis):
    seg = lax.axis_index("segment")
    share = weight.shape[axis] // 2
    mine = lax.dynamic_slice_in_dim(weight, seg * share, share, axis)
    fetched = swapped(mine, "mp")
    return lax.all_gather(fetched, "segment", axis=axis, tiled=True)


def route(ids, experts, per_device, offset):
    rows = ids.shape[0]
    lanes = jnp.arange(experts, dtype=jnp.int32)
    hot = jnp.any(ids[:, :, None] == lanes[None, None, :], axis=1)
    hot_b = hot.astype(BF16)
    below = (jnp.arange(rows)[:, None] > jnp.arange(rows)[None, :]).astype(BF16)
    slot = dot(below, hot_b)
    code = jnp.where(hot, slot, -1.0).astype(BF16)
    columns = jnp.arange(experts * per_device, dtype=jnp.int32)
    spread = (lanes[:, None] == (columns // per_device)[None, :]).astype(BF16)
    wide = dot(code, spread)
    wanted = (offset + columns % per_device).astype(F32)
    return hot, wide == wanted[None, :], spread


def layer(pieces, taps, gain, bias, dilation, count):
    reach = (taps.shape[0] - 1) * dilation
    mixed = jnp.zeros((count, pieces.shape[1]), F32)
    for j in range(taps.shape[0]):
        start = reach - j * dilation
        mixed = mixed + taps[j] * pieces[start : start + count]
    channels = pieces.shape[1]
    center = jnp.sum(mixed, axis=1, keepdims=True) / channels
    spread = jnp.sum(mixed * mixed, axis=1, keepdims=True) / channels - center * center
    normed = (mixed - center) * lax.rsqrt(spread + 1e-06)
    return (pieces[reach:] + normed * gain + bias).astype(BF16)


def on_device(
    start_state,
    expert_ids,
    norm_gain,
    w_router,
    w_gate,
    w_up,
    w_down,
    w_in,
    trans_taps,
    dw_kernels,
    ln_gain,
    ln_bias,
    w_out,
):
    seg = lax.axis_index("segment")
    mp = lax.axis_index("mp")
    rows, half = start_state.shape
    experts = w_router.shape[1]
    steps, _, topk = expert_ids.shape
    layers, kernel, _ = dw_kernels.shape
    capacity = min(rows, max(2, 2 * rows * topk // experts))
    parts = 4
    per_device = capacity // parts
    slots = experts * per_device
    offset = (mp * 2 + seg) * per_device
    depth = 2 * half
    share = rows // 2

    x = lax.all_gather(start_state, "mp", axis=1, tiled=True)
    gain_pair = lax.all_gather(norm_gain[None], "mp", axis=1, tiled=True)
    small = jnp.concatenate(
        [trans_taps, dw_kernels.reshape(layers * kernel, -1), ln_gain, ln_bias, w_out[None]], axis=0
    )
    small = jnp.concatenate([small, swapped(small, "mp")], axis=1)
    taps = small[:4]
    dw = small[4 : 4 + layers * kernel].reshape(layers, kernel, -1)
    rest = small[4 + layers * kernel :]
    gains, biases, wave = rest[:layers], rest[layers : 2 * layers], rest[2 * layers]

    gate = jnp.concatenate([w_gate[0], other_half(w_gate[0], 0)], axis=1)
    up = jnp.concatenate([w_up[0], other_half(w_up[0], 0)], axis=1)
    down = jnp.concatenate([w_down[0], other_half(w_down[0], 0)], axis=0)
    router_far = other_half(w_router, 0)
    router = jnp.where(
        mp == 0,
        jnp.concatenate([w_router, router_far], axis=0),
        jnp.concatenate([router_far, w_router], axis=0),
    )

    first = lax.axis_index("rows") == 0
    frames_back = 16
    voiced = []
    for step in range(steps):
        hot, placed, spread = route(expert_ids[step], experts, per_device, offset)
        xf = x.astype(F32)
        squares = jnp.sum(xf * xf, axis=1, keepdims=True)
        normed = (xf * lax.rsqrt(squares / depth + 1e-06) * gain_pair).astype(BF16)
        outgoing = lax.dot_general(
            placed.astype(BF16), normed, (((0,), (0,)), ((), ())), preferred_element_type=F32
        ).astype(BF16)
        received = lax.all_to_all(
            outgoing.reshape(experts, per_device, depth), "rows", split_axis=0, concat_axis=0, tiled=True
        )
        logits = dot(normed, router)
        squashed = jnp.where(hot, jax.nn.sigmoid(logits), 0.0)
        weights = squashed / jnp.sum(squashed, axis=1, keepdims=True)
        high = lax.reduce_precision(weights, 8, 7)
        low = weights - high
        pair = jnp.concatenate([high, low], axis=0).astype(BF16)
        both = jnp.concatenate([placed, placed], axis=0)
        combine = jnp.where(both, dot(pair, spread), 0.0).astype(BF16)

        flat = received.reshape(slots, depth)
        active = (jax.nn.silu(dot(flat, gate)) * dot(flat, up)).astype(BF16)
        answer = dot(active, down).astype(BF16)
        back = lax.all_to_all(
            answer.reshape(experts, per_device, depth), "rows", split_axis=0, concat_axis=0, tiled=True
        )
        mixed = dot(combine, back.reshape(slots, depth))
        partial = (mixed[:rows] + mixed[rows:]).astype(BF16)
        chip = lax.all_gather(partial, "segment", axis=0)
        chip = lax.dynamic_slice_in_dim(chip, seg * share, share, 1).astype(F32)
        chip = (chip[0] + chip[1]).astype(BF16)
        total = lax.all_gather(chip, "mp", axis=0).astype(F32)
        mine = lax.dynamic_slice_in_dim(x, seg * share, share, 0).astype(F32)
        fresh = (mine + (total[0] + total[1])).astype(BF16)
        x = lax.all_gather(fresh, "segment", axis=0, tiled=True)

        own = dot(x, w_in).astype(BF16)
        frames = jnp.concatenate([own, swapped(own, "mp")], axis=1)
        earlier = passed_along(frames[-frames_back:])
        frames = jnp.concatenate([earlier, frames], axis=0).astype(F32)
        now, before = frames[1:], frames[:-1]
        even = taps[0] * now + taps[2] * before
        odd = taps[1] * now + taps[3] * before
        signal = jnp.stack([even, odd], axis=1).reshape(-1, frames.shape[1]).astype(BF16)
        length = 2 * rows
        needed = length + sum((kernel - 1) * 3**i for i in range(layers))
        signal = signal[-needed:]
        for i in range(layers):
            needed -= (kernel - 1) * 3**i
            signal = layer(signal.astype(F32), dw[i], gains[i], biases[i], 3**i, needed)
            halo = needed - length
            if halo:
                head = jnp.where(first, jnp.zeros_like(signal[:halo]), signal[:halo])
                signal = jnp.concatenate([head, signal[halo:]], axis=0)
        voiced.append(jnp.sum(signal.astype(F32) * wave, axis=1))
    audio = jnp.stack(voiced, axis=0)
    audio = jnp.where(seg == 0, jnp.zeros_like(audio), audio)[None]
    state = lax.dynamic_slice_in_dim(x, mp * half, half, 1)
    return state, audio


def solution(mesh):
    return jax.shard_map(
        on_device,
        mesh=mesh,
        in_specs=(
            P("rows", "mp"),
            P(None, "rows", None),
            P("mp"),
            P("mp", None),
            P("rows", None, "mp"),
            P("rows", None, "mp"),
            P("rows", "mp", None),
            P(None, "mp"),
            P(None, "mp"),
            P(None, None, "mp"),
            P(None, "mp"),
            P(None, "mp"),
            P("mp"),
        ),
        out_specs=(P("rows", "mp"), P("segment", None, "rows")),
        check_vma=False,
    )
```

```python
import functools

import jax
import jax.numpy as jnp
from jax import lax
from jax.experimental import pallas as pl
from jax.experimental.pallas import tpu as pltpu
from jax.sharding import PartitionSpec as P

BF16 = jnp.bfloat16
F32 = jnp.float32
QUARTERS = 4
BACK = 16
LANES = 128
VMEM = pltpu.VMEM
HBM = pltpu.HBM
SMEM = pltpu.SMEM


def dot(a, b):
    return jnp.dot(a, b, preferred_element_type=F32)


def dot_t(a, b):
    return lax.dot_general(a, b, (((1,), (1,)), ((), ())), preferred_element_type=F32)


def swapped(block, axis):
    return lax.ppermute(block, axis, [(0, 1), (1, 0)])


def passed_along(block):
    count = lax.axis_size("rows")
    return lax.ppermute(block, "rows", [(i, i + 1) for i in range(count - 1)])


def call(kernel, outs, *args, scratch=(), flops=0, places=None, out_places=None, grant=40):
    single = not isinstance(outs, (list, tuple))
    listed = [outs] if single else list(outs)
    moved = sum(a.size * a.dtype.itemsize for a in args)
    moved += sum(o.size * o.dtype.itemsize for o in listed)
    places = places or [VMEM] * len(args)
    out_places = out_places or [VMEM] * len(listed)
    specs = [pl.BlockSpec(memory_space=p) for p in places]
    out_specs = [pl.BlockSpec(memory_space=p) for p in out_places]
    return pl.pallas_call(
        kernel,
        out_shape=outs,
        in_specs=specs,
        out_specs=out_specs[0] if single else out_specs,
        scratch_shapes=list(scratch),
        compiler_params=pltpu.CompilerParams(vmem_limit_bytes=grant * 1024 * 1024),
        cost_estimate=pl.CostEstimate(flops=flops, bytes_accessed=moved, transcendentals=0),
    )(*args)


def shaped(shape, dtype):
    return jax.ShapeDtypeStruct(shape, dtype)


def pack_kernel(seg_ref, state_ref, gain_ref, gate_ref, up_ref, out_ref):
    rows, half = state_ref.shape
    top = rows // 2
    share = gate_ref.shape[0] // 2
    out_ref[:top, :half] = state_ref[:top, :]
    out_ref[:top, half:] = state_ref[top:, :]
    gain = gain_ref[...]
    high = gain.astype(BF16)
    rest = gain - high.astype(F32)
    middle = rest.astype(BF16)
    low = (rest - middle.astype(F32)).astype(BF16)
    row = lax.broadcasted_iota(jnp.int32, (BACK, half), 0)
    terms = jnp.zeros((BACK, half), F32)
    for i, term in enumerate((high, middle, low)):
        terms = jnp.where(row == i, term.astype(F32), terms)
    out_ref[top : top + BACK, :half] = terms.astype(BF16)
    out_ref[top : top + BACK, half:] = terms.astype(BF16)
    place = top + BACK
    for ref in (gate_ref, up_ref):
        out_ref[place : place + share, :] = ref[pl.ds(seg_ref[0, 0] * share, share), :]
        place += share


def unpack_kernel(mp_ref, mine_ref, other_ref, x_ref, gain_ref):
    rows = x_ref.shape[0] // QUARTERS
    width = x_ref.shape[1]
    top = rows // 2
    ours = mp_ref[0, 0]
    for h in range(2):
        for q in range(2):
            for r in range(2):
                columns = slice((2 * r + q) * width, (2 * r + q + 1) * width)
                start = (2 * h + q) * rows + r * top
                mine = mine_ref[:top, columns].astype(F32)
                other = other_ref[:top, columns].astype(F32)
                x_ref[start : start + top, :] = jnp.where(ours == h, mine, other).astype(BF16)
            columns = slice(q * width, (q + 1) * width)
            mine = mine_ref[top : top + BACK, columns].astype(F32)
            other = other_ref[top : top + BACK, columns].astype(F32)
            terms = jnp.where(ours == h, mine, other)
            gain_ref[2 * h + q : 2 * h + q + 1, :] = (terms[0:1] + terms[1:2]) + terms[2:3]


def norm_kernel(depth, x_ref, gain_ref, pick_ref, out_ref, normed_ref, held_ref, sems):
    rows = x_ref.shape[0] // QUARTERS
    total = jnp.zeros((rows, 1), F32)
    for q in range(QUARTERS):
        part = x_ref[q * rows : (q + 1) * rows, :].astype(F32)
        total = total + jnp.sum(part * part, axis=1, keepdims=True)
    scale = lax.rsqrt(total / depth + 1e-06)
    for q in range(QUARTERS):
        part = x_ref[q * rows : (q + 1) * rows, :].astype(F32)
        normed_ref[q * rows : (q + 1) * rows, :] = (
            part * scale * gain_ref[q : q + 1, :]
        ).astype(BF16)
    normed = normed_ref[...]
    size = pick_ref.shape[0] // QUARTERS
    copies = []
    for i in range(QUARTERS):
        held_ref[i] = dot(pick_ref[i * size : (i + 1) * size, :], normed).astype(BF16)
        copy = pltpu.make_async_copy(
            held_ref.at[i], out_ref.at[pl.ds(i * size, size), :], sems.at[i]
        )
        copy.start()
        copies.append(copy)
    for copy in copies:
        copy.wait()


def weight_kernel(normed_ref, router_ref, hot_ref, spread_ref, mask_ref, out_ref):
    rows = normed_ref.shape[0] // QUARTERS
    width = normed_ref.shape[1]
    logits = jnp.zeros(hot_ref.shape, F32)
    for q in range(QUARTERS):
        logits = logits + dot(
            normed_ref[q * rows : (q + 1) * rows, :], router_ref[q * width : (q + 1) * width, :]
        )
    squashed = jnp.where(hot_ref[...] > 0.0, jax.nn.sigmoid(logits), 0.0)
    weights = squashed / jnp.sum(squashed, axis=1, keepdims=True)
    high = weights.astype(BF16)
    low = (weights - high.astype(F32)).astype(BF16)
    mask = mask_ref[...].astype(F32)
    out_ref[:rows, :] = (dot(high, spread_ref[...]) * mask).astype(BF16)
    out_ref[rows:, :] = (dot(low, spread_ref[...]) * mask).astype(BF16)


def expert_kernel(
    in_ref, gate, gate2, up, up2, down, down2, out_ref, wide_ref, held_ref, answer_ref, sems
):
    count, width = in_ref.shape
    slots = count // QUARTERS
    pieces = width // LANES
    loads = []
    for i, ref in enumerate((gate, gate2, up, up2, down, down2)):
        load = pltpu.make_async_copy(ref, held_ref.at[i], sems.at[i])
        load.start()
        loads.append(load)
    for c in range(pieces):
        wide_ref[c] = in_ref[:, c * LANES : (c + 1) * LANES].astype(F32)
    parts = []
    for q in range(QUARTERS):
        part = [wide_ref[c, pl.ds(q, slots, stride=QUARTERS), :] for c in range(pieces)]
        parts.append(jnp.concatenate(part, axis=1).astype(BF16))
    sums = []
    for i in range(4):
        loads[i].wait()
        sums.append(
            sum(dot_t(parts[q], held_ref[i, :, q * width : (q + 1) * width]) for q in range(QUARTERS))
        )
    first = (sums[0] / (1.0 + jnp.exp(-sums[0])) * sums[2]).astype(BF16)
    second = (sums[1] / (1.0 + jnp.exp(-sums[1])) * sums[3]).astype(BF16)
    loads[4].wait()
    loads[5].wait()
    for q in range(QUARTERS):
        columns = slice(q * width, (q + 1) * width)
        answer = dot(first, held_ref[4, :, columns]) + dot(second, held_ref[5, :, columns])
        for c in range(pieces):
            wide_ref[c, pl.ds(q, slots, stride=QUARTERS), :] = answer[:, c * LANES : (c + 1) * LANES]
    stores = []
    size = count // QUARTERS
    for i in range(QUARTERS):
        span = slice(i * size, (i + 1) * size)
        for c in range(pieces):
            answer_ref[i, :, c * LANES : (c + 1) * LANES] = wide_ref[c, span, :].astype(BF16)
        store = pltpu.make_async_copy(
            answer_ref.at[i], out_ref.at[pl.ds(i * size, size), :], sems.at[6 + i]
        )
        store.start()
        stores.append(store)
    for store in stores:
        store.wait()


def combine_kernel(weight_ref, back_ref, out_ref):
    rows = weight_ref.shape[0] // 2
    weights = weight_ref[...].astype(F32)
    lane = lax.broadcasted_iota(jnp.int32, weights.shape, 1) % QUARTERS
    chosen = jnp.concatenate(
        [jnp.where(lane == q, weights, 0.0).astype(BF16) for q in range(QUARTERS)], axis=0
    )
    mixed = dot(chosen, back_ref[...])
    for q in range(QUARTERS):
        start = 2 * q * rows
        out_ref[q * rows : (q + 1) * rows, :] = (
            mixed[start : start + rows] + mixed[start + rows : start + 2 * rows]
        ).astype(BF16)


def vocoder_kernel(layers, kernel, keep_ref, frame_ref, small_ref, out_ref, phase_ref, mixed_ref):
    count, channels = frame_ref.shape
    chunk = 256
    gains = 4 + layers * kernel
    blocks = [slice(c, c + chunk) for c in range(0, channels, chunk)]

    def back(value, frames):
        return value if frames == 0 else pltpu.roll(value, frames, 0)

    row = lax.broadcasted_iota(jnp.int32, (count, 1), 0)
    live = jnp.where(row < BACK, keep_ref[0, 0], 1.0)
    for block in blocks:
        now = frame_ref[:, block].astype(F32)
        before = back(now, 1)
        for p in range(2):
            phase_ref[p, :, block] = (
                small_ref[p : p + 1, block] * now + small_ref[p + 2 : p + 3, block] * before
            ).astype(BF16).astype(F32)
    for i in range(layers):
        dilation = 3**i
        sums = [jnp.zeros((count, 1), F32) for _ in range(2)]
        powers = [jnp.zeros((count, 1), F32) for _ in range(2)]
        for block in blocks:
            phases = [phase_ref[0, :, block], phase_ref[1, :, block]]
            for p in range(2):
                mixed = jnp.zeros((count, chunk), F32)
                for j in range(kernel):
                    at = p - j * dilation
                    tap = small_ref[4 + i * kernel + j : 5 + i * kernel + j, block]
                    mixed = mixed + tap * back(phases[at % 2], -(at // 2))
                mixed_ref[p, :, block] = mixed
                sums[p] = sums[p] + jnp.sum(mixed, axis=1, keepdims=True)
                powers[p] = powers[p] + jnp.sum(mixed * mixed, axis=1, keepdims=True)
        for p in range(2):
            center = sums[p] / channels
            scale = lax.rsqrt(powers[p] / channels - center * center + 1e-06)
            voice = jnp.zeros((count, 1), F32)
            for block in blocks:
                gain = small_ref[gains + i : gains + i + 1, block]
                bias = small_ref[gains + layers + i : gains + layers + i + 1, block]
                fresh = (
                    phase_ref[p, :, block]
                    + (mixed_ref[p, :, block] - center) * scale * gain
                    + bias
                )
                fresh = fresh.astype(BF16).astype(F32)
                if i < layers - 1:
                    phase_ref[p, :, block] = fresh * live
                else:
                    wave = small_ref[gains + 2 * layers : gains + 2 * layers + 1, block]
                    voice = voice + jnp.sum(fresh * wave, axis=1, keepdims=True)
            if i == layers - 1:
                out_ref[:, p : p + 1] = voice[BACK:, :]


def other_half(weight, axis):
    seg = lax.axis_index("segment")
    share = weight.shape[axis] // 2
    mine = lax.dynamic_slice_in_dim(weight, seg * share, share, axis)
    return swapped(mine, "mp")


def joined(share, axis):
    return lax.all_gather(share, "segment", axis=axis, tiled=True)


def route_kernel(per_device, offset_ref, ids_ref, *out_refs):
    steps, topk, wide = ids_ref.shape
    rows = wide // QUARTERS
    spread_ref = out_refs[-1]
    experts, columns = spread_ref.shape
    group = per_device * QUARTERS

    def iota(shape, axis):
        return lax.broadcasted_iota(jnp.int32, shape, axis)

    def ones(condition):
        return jnp.where(condition, 1.0, 0.0)

    name = iota((experts, wide), 0)
    ahead, behind = iota((wide, wide), 0), iota((wide, wide), 1)
    same = ahead // rows == behind // rows
    below = ones(same & (ahead % rows < behind % rows)).astype(BF16)
    unit = ones(iota((rows, wide), 0) == iota((rows, wide), 1)).astype(BF16)
    spread = ones(iota((experts, columns), 1) // group == iota((experts, columns), 0)).astype(BF16)
    tall = ones(iota((columns, experts), 0) // group == iota((columns, experts), 1)).astype(BF16)
    slot_row = iota((1, columns), 1) // QUARTERS % per_device
    column = iota((columns, wide), 0)
    slot_column = (column // QUARTERS % per_device).astype(F32)
    own = column % QUARTERS == iota((columns, wide), 1) // rows
    spread_ref[...] = spread
    for s in range(steps):
        hot_ref, mask_ref, pick_ref = out_refs[3 * s : 3 * s + 3]
        named = jnp.zeros((experts, wide), F32)
        for k in range(topk):
            named = named + ones(ids_ref[s, k : k + 1, :] == name)
        earlier = dot(named.astype(BF16), below)
        code = jnp.where(named > 0.0, earlier - offset_ref[0, 0], -64.0).astype(BF16)
        upright = dot_t(unit, code)
        hot_ref[...] = ones(upright > -32.0)
        mask_ref[...] = ones(dot(upright.astype(BF16), spread) == slot_row.astype(F32)).astype(BF16)
        pick_ref[...] = ones((dot(tall, code) == slot_column) & own).astype(BF16)


def on_device(
    start_state,
    expert_ids,
    norm_gain,
    w_router,
    w_gate,
    w_up,
    w_down,
    w_in,
    trans_taps,
    dw_kernels,
    ln_gain,
    ln_bias,
    w_out,
):
    seg = lax.axis_index("segment")
    mp = lax.axis_index("mp")
    rows, half = start_state.shape
    experts = w_router.shape[1]
    steps, _, topk = expert_ids.shape
    layers, kernel, channels = dw_kernels.shape
    channels = 2 * channels
    capacity = min(rows, max(2, 2 * rows * topk // experts))
    per_device = capacity // 4
    slots = experts * per_device
    offset = ((mp * 2 + seg) * per_device).astype(F32)
    depth = 2 * half
    width = depth // QUARTERS
    share = 2 * rows

    def ordered(mine, other, axis):
        return jnp.where(
            mp == 0,
            jnp.concatenate([mine, other], axis=axis),
            jnp.concatenate([other, mine], axis=axis),
        )

    gate, up, down = w_gate[0].T, w_up[0].T, w_down[0]
    part = gate.shape[0] // 2
    top = rows // 2
    packed = call(
        pack_kernel,
        shaped((top + BACK + 2 * part, depth), BF16),
        seg.astype(jnp.int32).reshape(1, 1),
        start_state,
        norm_gain[None],
        gate,
        up,
        places=[SMEM, VMEM, VMEM, VMEM, VMEM],
    )
    sent = swapped(packed, "mp")
    x, gain = call(
        unpack_kernel,
        (shaped((QUARTERS * rows, width), BF16), shaped((QUARTERS, width), F32)),
        mp.astype(jnp.int32).reshape(1, 1),
        packed[: top + BACK],
        sent[: top + BACK],
        places=[SMEM, VMEM, VMEM],
    )
    gate_share = sent[top + BACK : top + BACK + part]
    up_share = sent[top + BACK + part :]
    small = jnp.concatenate(
        [trans_taps, dw_kernels.reshape(layers * kernel, -1), ln_gain, ln_bias, w_out[None]], axis=0
    )
    small = jnp.concatenate([small, swapped(small, "mp")], axis=1)
    down_share = other_half(down, 0)
    router_share = other_half(w_router, 0)
    keep = jnp.where(lax.axis_index("rows") == 0, 0.0, 1.0).astype(F32).reshape(1, 1)

    turned = expert_ids.transpose(0, 2, 1)
    columns = slots * QUARTERS
    made = call(
        functools.partial(route_kernel, per_device),
        [
            shaped((rows, experts), F32),
            shaped((rows, columns), BF16),
            shaped((columns, QUARTERS * rows), BF16),
        ]
        * steps
        + [shaped((experts, columns), BF16)],
        offset.reshape(1, 1),
        jnp.concatenate([turned] * QUARTERS, axis=2),
        flops=4 * steps * columns * experts * QUARTERS * rows,
    )
    spread = made[-1]
    hots, masks, picks = made[:-1:3], made[1:-1:3], made[2:-1:3]
    gate2 = up2 = down2 = router = None
    frames = None
    voiced = []

    def voice(frames):
        return call(
            functools.partial(vocoder_kernel, layers, kernel),
            shaped((rows, 2), F32),
            keep,
            frames,
            small,
            scratch=[
                pltpu.VMEM((2, rows + BACK, channels), F32),
                pltpu.VMEM((2, rows + BACK, channels), F32),
            ],
            flops=20 * rows * channels * kernel,
        )

    for step in range(steps):
        hot, mask, pick = hots[step], masks[step], picks[step]
        outgoing, normed = call(
            functools.partial(norm_kernel, depth),
            (shaped((slots * QUARTERS, width), BF16), shaped((QUARTERS * rows, width), BF16)),
            x,
            gain,
            pick,
            scratch=[
                pltpu.VMEM((QUARTERS, slots, width), BF16),
                pltpu.SemaphoreType.DMA((QUARTERS,)),
            ],
            out_places=[HBM, VMEM],
            grant=60,
            flops=2 * slots * QUARTERS * QUARTERS * rows * width,
        )
        received = lax.all_to_all(
            outgoing.reshape(experts, per_device * QUARTERS, width),
            "rows",
            split_axis=0,
            concat_axis=0,
            tiled=True,
        )
        if step == 0:
            gate2, up2, down2 = joined(gate_share, 0), joined(up_share, 0), joined(down_share, 0)
            router = ordered(w_router, joined(router_share, 0), 0)
        weights = call(
            weight_kernel,
            shaped((2 * rows, slots * QUARTERS), BF16),
            normed,
            router,
            hot,
            spread,
            mask,
            flops=4 * rows * experts * (depth + slots * QUARTERS),
        )
        if frames is not None:
            received, frames, weights = lax.optimization_barrier((received, frames, weights))
        answer = call(
            expert_kernel,
            shaped((slots * QUARTERS, width), BF16),
            received.reshape(slots * QUARTERS, width),
            gate,
            gate2,
            up,
            up2,
            down,
            down2,
            scratch=[
                pltpu.VMEM((width // LANES, slots * QUARTERS, LANES), F32),
                pltpu.VMEM((6,) + gate.shape, BF16),
                pltpu.VMEM((QUARTERS, slots, width), BF16),
                pltpu.SemaphoreType.DMA((6 + QUARTERS,)),
            ],
            places=[VMEM] + [HBM] * 6,
            out_places=[HBM],
            grant=60,
            flops=12 * slots * depth * w_gate.shape[2],
        )
        back = lax.all_to_all(
            answer.reshape(experts, per_device * QUARTERS, width),
            "rows",
            split_axis=0,
            concat_axis=0,
            tiled=True,
        )
        if frames is not None:
            sound = voice(frames)
            back, sound = lax.optimization_barrier((back, sound))
            voiced.append(sound)
        partial = call(
            combine_kernel,
            shaped((QUARTERS * rows, width), BF16),
            weights,
            back.reshape(slots * QUARTERS, width),
            flops=4 * slots * QUARTERS * QUARTERS * rows * width,
        )
        chip = lax.all_gather(partial, "segment", axis=0)
        chip = lax.dynamic_slice_in_dim(chip, seg * share, share, 1).astype(F32)
        chip = (chip[0] + chip[1]).astype(BF16)
        total = lax.all_gather(chip, "mp", axis=0).astype(F32)
        mine = lax.dynamic_slice_in_dim(x, seg * share, share, 0).astype(F32)
        fresh = (mine + (total[0] + total[1])).astype(BF16)
        x = lax.all_gather(fresh, "segment", axis=0, tiled=True)

        own = sum(
            dot(x[q * rows : (q + 1) * rows], w_in[q * width : (q + 1) * width])
            for q in range(QUARTERS)
        ).astype(BF16)
        frames = jnp.concatenate([own, swapped(own, "mp")], axis=1)
        frames = jnp.concatenate([passed_along(frames[-BACK:]), frames], axis=0)
    voiced.append(voice(frames))
    audio = jnp.stack([v.reshape(2 * rows) for v in voiced], axis=0)
    audio = jnp.where(seg == 0, jnp.zeros_like(audio), audio)[None]
    state = lax.dynamic_slice_in_dim(x, mp * share, share, 0)
    state = jnp.concatenate([state[:rows], state[rows:]], axis=1)
    return state, audio


def solution(mesh):
    return jax.shard_map(
        on_device,
        mesh=mesh,
        in_specs=(
            P("rows", "mp"),
            P(None, "rows", None),
            P("mp"),
            P("mp", None),
            P("rows", None, "mp"),
            P("rows", None, "mp"),
            P("rows", "mp", None),
            P(None, "mp"),
            P(None, "mp"),
            P(None, None, "mp"),
            P(None, "mp"),
            P(None, "mp"),
            P("mp"),
        ),
        out_specs=(P("rows", "mp"), P("segment", None, "rows")),
        check_vma=False,
    )
```

```python
import functools

import jax
import jax.numpy as jnp
from jax import lax
from jax.experimental import pallas as pl
from jax.experimental.pallas import tpu as pltpu
from jax.sharding import PartitionSpec as P

BF16 = jnp.bfloat16
F32 = jnp.float32
QUARTERS = 4
BACK = 16
LANES = 128
VMEM = pltpu.VMEM
SMEM = pltpu.SMEM


def dot(a, b):
    return jnp.dot(a, b, preferred_element_type=F32)


def dot_t(a, b):
    return lax.dot_general(a, b, (((1,), (1,)), ((), ())), preferred_element_type=F32)


def swapped(block, axis):
    return lax.ppermute(block, axis, [(0, 1), (1, 0)])


def voiced_swap(block):
    return lax.ppermute(block, ("segment", "mp"), [(2, 3), (3, 2)])


def voiced_pass(block):
    count = lax.axis_size("rows")
    route = [(count + i, count + i + 1) for i in range(count - 1)]
    return lax.ppermute(block, ("segment", "rows"), route)


def call(kernel, outs, *args, scratch=(), flops=0, places=None, grant=10):
    single = not isinstance(outs, (list, tuple))
    listed = [outs] if single else list(outs)
    moved = sum(a.size * a.dtype.itemsize for a in args)
    moved += sum(o.size * o.dtype.itemsize for o in listed)
    places = places or [VMEM] * len(args)
    specs = [pl.BlockSpec(memory_space=p) for p in places]
    out_specs = [pl.BlockSpec(memory_space=VMEM)] * len(listed)
    return pl.pallas_call(
        kernel,
        out_shape=outs,
        in_specs=specs,
        out_specs=out_specs[0] if single else out_specs,
        scratch_shapes=list(scratch),
        compiler_params=pltpu.CompilerParams(vmem_limit_bytes=grant * 1024 * 1024),
        cost_estimate=pl.CostEstimate(flops=flops, bytes_accessed=moved, transcendentals=0),
    )(*args)


def shaped(shape, dtype):
    return jax.ShapeDtypeStruct(shape, dtype)


def pack_kernel(seg_ref, state_ref, gain_ref, gate_ref, up_ref, down_ref, out_ref):
    rows, half = state_ref.shape
    top = rows // 2
    share = gate_ref.shape[0] // 2
    out_ref[:top, :half] = state_ref[:top, :]
    out_ref[:top, half:] = state_ref[top:, :]
    gain = gain_ref[...]
    high = gain.astype(BF16)
    rest = gain - high.astype(F32)
    middle = rest.astype(BF16)
    low = (rest - middle.astype(F32)).astype(BF16)
    row = lax.broadcasted_iota(jnp.int32, (BACK, half), 0)
    terms = jnp.zeros((BACK, half), F32)
    for i, term in enumerate((high, middle, low)):
        terms = jnp.where(row == i, term.astype(F32), terms)
    out_ref[top : top + BACK, :half] = terms.astype(BF16)
    out_ref[top : top + BACK, half:] = terms.astype(BF16)
    place = top + BACK
    for ref in (gate_ref, up_ref, down_ref):
        out_ref[place : place + share, :] = ref[pl.ds(seg_ref[0, 0] * share, share), :]
        place += share


def unpack_kernel(mp_ref, mine_ref, other_ref, x_ref, gain_ref):
    rows = x_ref.shape[0] // QUARTERS
    width = x_ref.shape[1]
    top = rows // 2
    ours = mp_ref[0, 0]
    for h in range(2):
        for q in range(2):
            for r in range(2):
                columns = slice((2 * r + q) * width, (2 * r + q + 1) * width)
                start = (2 * h + q) * rows + r * top
                mine = mine_ref[:top, columns].astype(F32)
                other = other_ref[:top, columns].astype(F32)
                x_ref[start : start + top, :] = jnp.where(ours == h, mine, other).astype(BF16)
            columns = slice(q * width, (q + 1) * width)
            mine = mine_ref[top : top + BACK, columns].astype(F32)
            other = other_ref[top : top + BACK, columns].astype(F32)
            terms = jnp.where(ours == h, mine, other)
            gain_ref[2 * h + q : 2 * h + q + 1, :] = (terms[0:1] + terms[1:2]) + terms[2:3]


def norm_kernel(depth, x_ref, gain_ref, pick_ref, out_ref, normed_ref):
    rows = x_ref.shape[0] // QUARTERS
    total = jnp.zeros((rows, 1), F32)
    for q in range(QUARTERS):
        part = x_ref[q * rows : (q + 1) * rows, :].astype(F32)
        total = total + jnp.sum(part * part, axis=1, keepdims=True)
    scale = lax.rsqrt(total / depth + 1e-06)
    for q in range(QUARTERS):
        part = x_ref[q * rows : (q + 1) * rows, :].astype(F32)
        normed_ref[q * rows : (q + 1) * rows, :] = (
            part * scale * gain_ref[q : q + 1, :]
        ).astype(BF16)
    out_ref[...] = dot(pick_ref[...], normed_ref[...]).astype(BF16)


def weight_kernel(normed_ref, router_ref, hot_ref, spread_ref, mask_ref, out_ref):
    rows = normed_ref.shape[0] // QUARTERS
    width = normed_ref.shape[1]
    logits = jnp.zeros(hot_ref.shape, F32)
    for q in range(QUARTERS):
        logits = logits + dot(
            normed_ref[q * rows : (q + 1) * rows, :], router_ref[q * width : (q + 1) * width, :]
        )
    squashed = jnp.where(hot_ref[...] > 0.0, jax.nn.sigmoid(logits), 0.0)
    weights = squashed / jnp.sum(squashed, axis=1, keepdims=True)
    high = weights.astype(BF16)
    low = (weights - high.astype(F32)).astype(BF16)
    mask = mask_ref[...].astype(F32)
    out_ref[:rows, :] = (dot(high, spread_ref[...]) * mask).astype(BF16)
    out_ref[rows:, :] = (dot(low, spread_ref[...]) * mask).astype(BF16)


def expert_kernel(
    in_ref, gate_ref, gate2_ref, up_ref, up2_ref, down_ref, down2_ref, out_ref, wide_ref
):
    count, width = in_ref.shape
    slots = count // QUARTERS
    lanes = gate_ref.shape[0]
    pieces = width // LANES
    for c in range(pieces):
        wide_ref[c] = in_ref[:, c * LANES : (c + 1) * LANES].astype(F32)
    sums = [jnp.zeros((slots, lanes), F32) for _ in range(4)]
    for q in range(QUARTERS):
        part = jnp.concatenate(
            [wide_ref[c, pl.ds(q, slots, stride=QUARTERS), :] for c in range(pieces)], axis=1
        ).astype(BF16)
        columns = slice(q * width, (q + 1) * width)
        for i, ref in enumerate((gate_ref, gate2_ref, up_ref, up2_ref)):
            sums[i] = sums[i] + dot_t(part, ref[:, columns])
    first = (sums[0] / (1.0 + jnp.exp(-sums[0])) * sums[2]).astype(BF16)
    second = (sums[1] / (1.0 + jnp.exp(-sums[1])) * sums[3]).astype(BF16)
    for q in range(QUARTERS):
        columns = slice(q * width, (q + 1) * width)
        answer = dot(first, down_ref[:, columns]) + dot(second, down2_ref[:, columns])
        for c in range(pieces):
            wide_ref[c, pl.ds(q, slots, stride=QUARTERS), :] = answer[:, c * LANES : (c + 1) * LANES]
    for c in range(pieces):
        out_ref[:, c * LANES : (c + 1) * LANES] = wide_ref[c].astype(BF16)


def combine_kernel(weight_ref, back_ref, out_ref):
    rows = weight_ref.shape[0] // 2
    weights = weight_ref[...].astype(F32)
    lane = lax.broadcasted_iota(jnp.int32, weights.shape, 1) % QUARTERS
    chosen = jnp.concatenate(
        [jnp.where(lane == q, weights, 0.0).astype(BF16) for q in range(QUARTERS)], axis=0
    )
    mixed = dot(chosen, back_ref[...])
    for q in range(QUARTERS):
        start = 2 * q * rows
        out_ref[q * rows : (q + 1) * rows, :] = (
            mixed[start : start + rows] + mixed[start + rows : start + 2 * rows]
        ).astype(BF16)


def vocoder_kernel(layers, kernel, keep_ref, frame_ref, small_ref, out_ref, phase_ref, mixed_ref):
    count, channels = frame_ref.shape
    chunk = 256
    gains = 4 + layers * kernel
    blocks = [slice(c, c + chunk) for c in range(0, channels, chunk)]

    def back(value, frames):
        return value if frames == 0 else pltpu.roll(value, frames, 0)

    row = lax.broadcasted_iota(jnp.int32, (count, 1), 0)
    live = jnp.where(row < BACK, keep_ref[0, 0], 1.0)
    for block in blocks:
        now = frame_ref[:, block].astype(F32)
        before = back(now, 1)
        for p in range(2):
            phase_ref[p, :, block] = (
                small_ref[p : p + 1, block] * now + small_ref[p + 2 : p + 3, block] * before
            ).astype(BF16).astype(F32)
    for i in range(layers):
        dilation = 3**i
        sums = [jnp.zeros((count, 1), F32) for _ in range(2)]
        powers = [jnp.zeros((count, 1), F32) for _ in range(2)]
        for block in blocks:
            phases = [phase_ref[0, :, block], phase_ref[1, :, block]]
            for p in range(2):
                mixed = jnp.zeros((count, chunk), F32)
                for j in range(kernel):
                    at = p - j * dilation
                    tap = small_ref[4 + i * kernel + j : 5 + i * kernel + j, block]
                    mixed = mixed + tap * back(phases[at % 2], -(at // 2))
                mixed_ref[p, :, block] = mixed
                sums[p] = sums[p] + jnp.sum(mixed, axis=1, keepdims=True)
                powers[p] = powers[p] + jnp.sum(mixed * mixed, axis=1, keepdims=True)
        for p in range(2):
            center = sums[p] / channels
            scale = lax.rsqrt(powers[p] / channels - center * center + 1e-06)
            voice = jnp.zeros((count, 1), F32)
            for block in blocks:
                gain = small_ref[gains + i : gains + i + 1, block]
                bias = small_ref[gains + layers + i : gains + layers + i + 1, block]
                fresh = (
                    phase_ref[p, :, block]
                    + (mixed_ref[p, :, block] - center) * scale * gain
                    + bias
                )
                fresh = fresh.astype(BF16).astype(F32)
                if i < layers - 1:
                    phase_ref[p, :, block] = fresh * live
                else:
                    wave = small_ref[gains + 2 * layers : gains + 2 * layers + 1, block]
                    voice = voice + jnp.sum(fresh * wave, axis=1, keepdims=True)
            if i == layers - 1:
                out_ref[:, p : p + 1] = voice[BACK:, :]


def other_half(weight, axis):
    seg = lax.axis_index("segment")
    share = weight.shape[axis] // 2
    mine = lax.dynamic_slice_in_dim(weight, seg * share, share, axis)
    return swapped(mine, "mp")


def joined(share, axis):
    return lax.all_gather(share, "segment", axis=axis, tiled=True)


def route_kernel(per_device, offset_ref, ids_ref, *out_refs):
    steps, topk, wide = ids_ref.shape
    rows = wide // QUARTERS
    spread_ref = out_refs[-1]
    experts, columns = spread_ref.shape
    group = per_device * QUARTERS

    def iota(shape, axis):
        return lax.broadcasted_iota(jnp.int32, shape, axis)

    def ones(condition):
        return jnp.where(condition, 1.0, 0.0)

    name = iota((experts, wide), 0)
    ahead, behind = iota((wide, wide), 0), iota((wide, wide), 1)
    same = ahead // rows == behind // rows
    below = ones(same & (ahead % rows < behind % rows)).astype(BF16)
    unit = ones(iota((rows, wide), 0) == iota((rows, wide), 1)).astype(BF16)
    spread = ones(iota((experts, columns), 1) // group == iota((experts, columns), 0)).astype(BF16)
    tall = ones(iota((columns, experts), 0) // group == iota((columns, experts), 1)).astype(BF16)
    slot_row = iota((1, columns), 1) // QUARTERS % per_device
    column = iota((columns, wide), 0)
    slot_column = (column // QUARTERS % per_device).astype(F32)
    own = column % QUARTERS == iota((columns, wide), 1) // rows
    spread_ref[...] = spread
    for s in range(steps):
        hot_ref, mask_ref, pick_ref = out_refs[3 * s : 3 * s + 3]
        named = jnp.zeros((experts, wide), F32)
        for k in range(topk):
            named = named + ones(ids_ref[s, k : k + 1, :] == name)
        earlier = dot(named.astype(BF16), below)
        code = jnp.where(named > 0.0, earlier - offset_ref[0, 0], -64.0).astype(BF16)
        upright = dot_t(unit, code)
        hot_ref[...] = ones(upright > -32.0)
        mask_ref[...] = ones(dot(upright.astype(BF16), spread) == slot_row.astype(F32)).astype(BF16)
        pick_ref[...] = ones((dot(tall, code) == slot_column) & own).astype(BF16)


def on_device(
    start_state,
    expert_ids,
    norm_gain,
    w_router,
    w_gate,
    w_up,
    w_down,
    w_in,
    trans_taps,
    dw_kernels,
    ln_gain,
    ln_bias,
    w_out,
):
    seg = lax.axis_index("segment")
    mp = lax.axis_index("mp")
    rows, half = start_state.shape
    experts = w_router.shape[1]
    steps, _, topk = expert_ids.shape
    layers, kernel, channels = dw_kernels.shape
    channels = 2 * channels
    capacity = min(rows, max(2, 2 * rows * topk // experts))
    per_device = capacity // 4
    slots = experts * per_device
    offset = ((mp * 2 + seg) * per_device).astype(F32)
    depth = 2 * half
    width = depth // QUARTERS
    share = 2 * rows

    def ordered(mine, other, axis):
        return jnp.where(
            mp == 0,
            jnp.concatenate([mine, other], axis=axis),
            jnp.concatenate([other, mine], axis=axis),
        )

    gate, up, down = w_gate[0].T, w_up[0].T, w_down[0]
    part = gate.shape[0] // 2
    top = rows // 2
    packed = call(
        pack_kernel,
        shaped((top + BACK + 3 * part, depth), BF16),
        seg.astype(jnp.int32).reshape(1, 1),
        start_state,
        norm_gain[None],
        gate,
        up,
        down,
        places=[SMEM] + [VMEM] * 5,
        grant=14,
    )
    sent = swapped(packed, "mp")
    x, gain = call(
        unpack_kernel,
        (shaped((QUARTERS * rows, width), BF16), shaped((QUARTERS, width), F32)),
        mp.astype(jnp.int32).reshape(1, 1),
        packed[: top + BACK],
        sent[: top + BACK],
        places=[SMEM, VMEM, VMEM],
    )
    gate_share, up_share, down_share = (
        sent[top + BACK + i * part : top + BACK + (i + 1) * part] for i in range(3)
    )
    small = jnp.concatenate(
        [trans_taps, dw_kernels.reshape(layers * kernel, -1), ln_gain, ln_bias, w_out[None]], axis=0
    )
    small = jnp.concatenate([small, voiced_swap(small)], axis=1)
    router_share = other_half(w_router, 0)
    keep = jnp.where(lax.axis_index("rows") == 0, 0.0, 1.0).astype(F32).reshape(1, 1)

    turned = expert_ids.transpose(0, 2, 1)
    columns = slots * QUARTERS
    made = call(
        functools.partial(route_kernel, per_device),
        [
            shaped((rows, experts), F32),
            shaped((rows, columns), BF16),
            shaped((columns, QUARTERS * rows), BF16),
        ]
        * steps
        + [shaped((experts, columns), BF16)],
        offset.reshape(1, 1),
        jnp.concatenate([turned] * QUARTERS, axis=2),
        grant=16,
        flops=4 * steps * columns * experts * QUARTERS * rows,
    )
    spread = made[-1]
    hots, masks, picks = made[:-1:3], made[1:-1:3], made[2:-1:3]
    gate2 = up2 = down2 = router = None
    frames = None
    voiced = []

    def voice(frames):
        return call(
            functools.partial(vocoder_kernel, layers, kernel),
            shaped((rows, 2), F32),
            keep,
            frames,
            small,
            scratch=[
                pltpu.VMEM((2, rows + BACK, channels), F32),
                pltpu.VMEM((2, rows + BACK, channels), F32),
            ],
            flops=20 * rows * channels * kernel,
        )

    for step in range(steps):
        hot, mask, pick = hots[step], masks[step], picks[step]
        outgoing, normed = call(
            functools.partial(norm_kernel, depth),
            (shaped((slots * QUARTERS, width), BF16), shaped((QUARTERS * rows, width), BF16)),
            x,
            gain,
            pick,
            flops=2 * slots * QUARTERS * QUARTERS * rows * width,
        )
        received = lax.all_to_all(
            outgoing.reshape(experts, per_device * QUARTERS, width),
            "rows",
            split_axis=0,
            concat_axis=0,
            tiled=True,
        )
        if step == 0:
            gate2, up2, down2 = joined(gate_share, 0), joined(up_share, 0), joined(down_share, 0)
            router = ordered(w_router, joined(router_share, 0), 0)
        weights = call(
            weight_kernel,
            shaped((2 * rows, slots * QUARTERS), BF16),
            normed,
            router,
            hot,
            spread,
            mask,
            flops=4 * rows * experts * (depth + slots * QUARTERS),
        )
        if frames is not None:
            received, frames, weights = lax.optimization_barrier((received, frames, weights))
        answer = call(
            expert_kernel,
            shaped((slots * QUARTERS, width), BF16),
            received.reshape(slots * QUARTERS, width),
            gate,
            gate2,
            up,
            up2,
            down,
            down2,
            scratch=[pltpu.VMEM((width // LANES, slots * QUARTERS, LANES), F32)],
            grant=16,
            flops=12 * slots * depth * w_gate.shape[2],
        )
        back = lax.all_to_all(
            answer.reshape(experts, per_device * QUARTERS, width),
            "rows",
            split_axis=0,
            concat_axis=0,
            tiled=True,
        )
        if frames is not None:
            sound = voice(frames)
            back, sound = lax.optimization_barrier((back, sound))
            voiced.append(sound)
        partial = call(
            combine_kernel,
            shaped((QUARTERS * rows, width), BF16),
            weights,
            back.reshape(slots * QUARTERS, width),
            flops=4 * slots * QUARTERS * QUARTERS * rows * width,
        )
        chip = lax.all_gather(partial, "segment", axis=0)
        chip = lax.dynamic_slice_in_dim(chip, seg * share, share, 1).astype(F32)
        chip = (chip[0] + chip[1]).astype(BF16)
        total = lax.all_gather(chip, "mp", axis=0).astype(F32)
        mine = lax.dynamic_slice_in_dim(x, seg * share, share, 0).astype(F32)
        fresh = (mine + (total[0] + total[1])).astype(BF16)
        x = lax.all_gather(fresh, "segment", axis=0, tiled=True)

        own = sum(
            dot(x[q * rows : (q + 1) * rows], w_in[q * width : (q + 1) * width])
            for q in range(QUARTERS)
        ).astype(BF16)
        frames = jnp.concatenate([own, voiced_swap(own)], axis=1)
        frames = jnp.concatenate([voiced_pass(frames[-BACK:]), frames], axis=0)
    voiced.append(voice(frames))
    audio = jnp.stack([v.reshape(2 * rows) for v in voiced], axis=0)
    audio = jnp.where(seg == 0, jnp.zeros_like(audio), audio)[None]
    state = lax.dynamic_slice_in_dim(x, mp * share, share, 0)
    state = jnp.concatenate([state[:rows], state[rows:]], axis=1)
    return state, audio


def solution(mesh):
    return jax.shard_map(
        on_device,
        mesh=mesh,
        in_specs=(
            P("rows", "mp"),
            P(None, "rows", None),
            P("mp"),
            P("mp", None),
            P("rows", None, "mp"),
            P("rows", None, "mp"),
            P("rows", "mp", None),
            P(None, "mp"),
            P(None, "mp"),
            P(None, None, "mp"),
            P(None, "mp"),
            P(None, "mp"),
            P("mp"),
        ),
        out_specs=(P("rows", "mp"), P("segment", None, "rows")),
        check_vma=False,
    )
```

```python
import functools
import math

import jax
import jax.numpy as jnp
from jax import lax
from jax.experimental import pallas as pl
from jax.experimental.pallas import tpu as pltpu
from jax.sharding import PartitionSpec as P

BF16 = jnp.bfloat16
F32 = jnp.float32
QUARTERS = 4
BACK = 16
LANES = 128
VMEM = pltpu.VMEM
SMEM = pltpu.SMEM
HBM = pltpu.HBM


def dot(a, b):
    return jnp.dot(a, b, preferred_element_type=F32)


def dot_t(a, b):
    return lax.dot_general(a, b, (((1,), (1,)), ((), ())), preferred_element_type=F32)


def swapped(block, axis):
    return lax.ppermute(block, axis, [(0, 1), (1, 0)])


def voiced_swap(block):
    return lax.ppermute(block, ("segment", "mp"), [(2, 3), (3, 2)])


def voiced_pass(block):
    count = lax.axis_size("rows")
    route = [(count + i, count + i + 1) for i in range(count - 1)]
    return lax.ppermute(block, ("segment", "rows"), route)


def call(kernel, outs, *args, scratch=(), flops=0, places=None, grant=10):
    single = not isinstance(outs, (list, tuple))
    listed = [outs] if single else list(outs)
    moved = sum(math.prod(a.shape) * a.dtype.itemsize for a in list(args) + listed)
    places = places or [VMEM] * len(args)
    specs = [p if isinstance(p, pl.BlockSpec) else pl.BlockSpec(memory_space=p) for p in places]
    out_specs = [pl.BlockSpec(memory_space=getattr(o, "memory_space", VMEM)) for o in listed]
    out_specs = [
        s if s.memory_space in (VMEM, HBM) else pl.BlockSpec(memory_space=VMEM) for s in out_specs
    ]
    return pl.pallas_call(
        kernel,
        out_shape=outs,
        in_specs=specs,
        out_specs=out_specs[0] if single else out_specs,
        scratch_shapes=list(scratch),
        compiler_params=pltpu.CompilerParams(vmem_limit_bytes=grant * 1024 * 1024),
        cost_estimate=pl.CostEstimate(flops=flops, bytes_accessed=moved, transcendentals=0),
    )(*args)


def shaped(shape, dtype):
    return jax.ShapeDtypeStruct(shape, dtype)


def pack_kernel(
    seg_ref, state_ref, gain_ref, gate_ref, up_ref, down_ref, out_ref, head_out, head_ref, sems
):
    rows, half = state_ref.shape
    top = rows // 2
    share = gate_ref.shape[0] // 2
    copies = []
    from_row = pl.multiple_of(seg_ref[0, 0] * share, share)
    for i, ref in enumerate((gate_ref, up_ref, down_ref)):
        place = top + BACK + i * share
        copy = pltpu.make_async_copy(
            ref.at[pl.ds(from_row, share), :], out_ref.at[pl.ds(place, share), :], sems.at[i]
        )
        copy.start()
        copies.append(copy)
    head_ref[:top, :half] = state_ref[:top, :]
    head_ref[:top, half:] = state_ref[top:, :]
    gain = gain_ref[...]
    high = gain.astype(BF16)
    rest = gain - high.astype(F32)
    middle = rest.astype(BF16)
    low = (rest - middle.astype(F32)).astype(BF16)
    row = lax.broadcasted_iota(jnp.int32, (BACK, half), 0)
    terms = jnp.zeros((BACK, half), F32)
    for i, term in enumerate((high, middle, low)):
        terms = jnp.where(row == i, term.astype(F32), terms)
    head_ref[top:, :half] = terms.astype(BF16)
    head_ref[top:, half:] = terms.astype(BF16)
    copies.append(
        pltpu.make_async_copy(head_ref, out_ref.at[pl.ds(0, top + BACK), :], sems.at[3])
    )
    copies.append(pltpu.make_async_copy(head_ref, head_out, sems.at[4]))
    for copy in copies[3:]:
        copy.start()
    for copy in copies:
        copy.wait()


def unpack_kernel(mp_ref, mine_ref, other_ref, x_ref, gain_ref):
    rows = x_ref.shape[0] // QUARTERS
    width = x_ref.shape[1]
    top = rows // 2
    ours = mp_ref[0, 0]
    for h in range(2):
        for q in range(2):
            for r in range(2):
                columns = slice((2 * r + q) * width, (2 * r + q + 1) * width)
                start = (2 * h + q) * rows + r * top
                mine = mine_ref[:top, columns].astype(F32)
                other = other_ref[:top, columns].astype(F32)
                x_ref[start : start + top, :] = jnp.where(ours == h, mine, other).astype(BF16)
            columns = slice(q * width, (q + 1) * width)
            mine = mine_ref[top : top + BACK, columns].astype(F32)
            other = other_ref[top : top + BACK, columns].astype(F32)
            terms = jnp.where(ours == h, mine, other)
            gain_ref[2 * h + q : 2 * h + q + 1, :] = (terms[0:1] + terms[1:2]) + terms[2:3]


def norm_kernel(depth, x_ref, gain_ref, pick_ref, out_ref, normed_out, normed_ref, held_ref, sems):
    rows = x_ref.shape[0] // QUARTERS
    total = jnp.zeros((rows, 1), F32)
    for q in range(QUARTERS):
        part = x_ref[q * rows : (q + 1) * rows, :].astype(F32)
        total = total + jnp.sum(part * part, axis=1, keepdims=True)
    scale = lax.rsqrt(total / depth + 1e-06)
    for q in range(QUARTERS):
        part = x_ref[q * rows : (q + 1) * rows, :].astype(F32)
        normed_ref[q * rows : (q + 1) * rows, :] = (
            part * scale * gain_ref[q : q + 1, :]
        ).astype(BF16)
    copies = [pltpu.make_async_copy(normed_ref, normed_out, sems.at[QUARTERS])]
    copies[0].start()
    normed = normed_ref[...]
    size = pick_ref.shape[0] // QUARTERS
    for i in range(QUARTERS):
        held_ref[i] = dot(pick_ref[i * size : (i + 1) * size, :], normed).astype(BF16)
        copy = pltpu.make_async_copy(
            held_ref.at[i], out_ref.at[pl.ds(i * size, size), :], sems.at[i]
        )
        copy.start()
        copies.append(copy)
    for copy in copies:
        copy.wait()


def weight_kernel(normed_ref, router_ref, hot_ref, spread_ref, mask_ref, out_ref):
    rows = normed_ref.shape[0] // QUARTERS
    width = normed_ref.shape[1]
    logits = jnp.zeros(hot_ref.shape, F32)
    for q in range(QUARTERS):
        logits = logits + dot(
            normed_ref[q * rows : (q + 1) * rows, :], router_ref[q * width : (q + 1) * width, :]
        )
    squashed = jnp.where(hot_ref[...] > 0.0, jax.nn.sigmoid(logits), 0.0)
    weights = squashed / jnp.sum(squashed, axis=1, keepdims=True)
    high = weights.astype(BF16)
    low = (weights - high.astype(F32)).astype(BF16)
    mask = mask_ref[...].astype(F32)
    out_ref[:rows, :] = (dot(high, spread_ref[...]) * mask).astype(BF16)
    out_ref[rows:, :] = (dot(low, spread_ref[...]) * mask).astype(BF16)


def expert_kernel(
    in_ref,
    gate_ref,
    gate2_ref,
    up_ref,
    up2_ref,
    down_ref,
    down2_ref,
    out_ref,
    wide_ref,
    answer_ref,
    sems,
):
    count, width = in_ref.shape
    slots = count // QUARTERS
    lanes = gate_ref.shape[0]
    pieces = width // LANES
    for c in range(pieces):
        wide_ref[c] = in_ref[:, c * LANES : (c + 1) * LANES].astype(F32)
    sums = [jnp.zeros((slots, lanes), F32) for _ in range(4)]
    for q in range(QUARTERS):
        part = jnp.concatenate(
            [wide_ref[c, pl.ds(q, slots, stride=QUARTERS), :] for c in range(pieces)], axis=1
        ).astype(BF16)
        columns = slice(q * width, (q + 1) * width)
        for i, ref in enumerate((gate_ref, gate2_ref, up_ref, up2_ref)):
            sums[i] = sums[i] + dot_t(part, ref[:, columns])
    first = (sums[0] / (1.0 + jnp.exp(-sums[0])) * sums[2]).astype(BF16)
    second = (sums[1] / (1.0 + jnp.exp(-sums[1])) * sums[3]).astype(BF16)
    for q in range(QUARTERS):
        columns = slice(q * width, (q + 1) * width)
        answer = dot(first, down_ref[:, columns]) + dot(second, down2_ref[:, columns])
        for c in range(pieces):
            wide_ref[c, pl.ds(q, slots, stride=QUARTERS), :] = answer[:, c * LANES : (c + 1) * LANES]
    stores = []
    size = count // QUARTERS
    for i in range(QUARTERS):
        span = slice(i * size, (i + 1) * size)
        for c in range(pieces):
            answer_ref[i, :, c * LANES : (c + 1) * LANES] = wide_ref[c, span, :].astype(BF16)
        store = pltpu.make_async_copy(
            answer_ref.at[i], out_ref.at[pl.ds(i * size, size), :], sems.at[i]
        )
        store.start()
        stores.append(store)
    for store in stores:
        store.wait()


def combine_kernel(weight_ref, back_ref, out_ref):
    rows = weight_ref.shape[0] // 2
    weights = weight_ref[...].astype(F32)
    lane = lax.broadcasted_iota(jnp.int32, weights.shape, 1) % QUARTERS
    chosen = jnp.concatenate(
        [jnp.where(lane == q, weights, 0.0).astype(BF16) for q in range(QUARTERS)], axis=0
    )
    mixed = dot(chosen, back_ref[...])
    for q in range(QUARTERS):
        start = 2 * q * rows
        out_ref[q * rows : (q + 1) * rows, :] = (
            mixed[start : start + rows] + mixed[start + rows : start + 2 * rows]
        ).astype(BF16)


def vocoder_kernel(layers, kernel, keep_ref, frame_ref, small_ref, out_ref, phase_ref, mixed_ref):
    count, channels = frame_ref.shape
    chunk = 256
    gains = 4 + layers * kernel
    blocks = [slice(c, c + chunk) for c in range(0, channels, chunk)]

    def back(value, frames):
        return value if frames == 0 else pltpu.roll(value, frames, 0)

    row = lax.broadcasted_iota(jnp.int32, (count, 1), 0)
    live = jnp.where(row < BACK, keep_ref[0, 0], 1.0)
    for block in blocks:
        now = frame_ref[:, block].astype(F32)
        before = back(now, 1)
        for p in range(2):
            phase_ref[p, :, block] = (
                small_ref[p : p + 1, block] * now + small_ref[p + 2 : p + 3, block] * before
            ).astype(BF16).astype(F32)
    for i in range(layers):
        dilation = 3**i
        sums = [jnp.zeros((count, 1), F32) for _ in range(2)]
        powers = [jnp.zeros((count, 1), F32) for _ in range(2)]
        for block in blocks:
            phases = [phase_ref[0, :, block], phase_ref[1, :, block]]
            for p in range(2):
                mixed = jnp.zeros((count, chunk), F32)
                for j in range(kernel):
                    at = p - j * dilation
                    tap = small_ref[4 + i * kernel + j : 5 + i * kernel + j, block]
                    mixed = mixed + tap * back(phases[at % 2], -(at // 2))
                mixed_ref[p, :, block] = mixed
                sums[p] = sums[p] + jnp.sum(mixed, axis=1, keepdims=True)
                powers[p] = powers[p] + jnp.sum(mixed * mixed, axis=1, keepdims=True)
        for p in range(2):
            center = sums[p] / channels
            scale = lax.rsqrt(powers[p] / channels - center * center + 1e-06)
            voice = jnp.zeros((count, 1), F32)
            for block in blocks:
                gain = small_ref[gains + i : gains + i + 1, block]
                bias = small_ref[gains + layers + i : gains + layers + i + 1, block]
                fresh = (
                    phase_ref[p, :, block]
                    + (mixed_ref[p, :, block] - center) * scale * gain
                    + bias
                )
                fresh = fresh.astype(BF16).astype(F32)
                if i < layers - 1:
                    phase_ref[p, :, block] = fresh * live
                else:
                    wave = small_ref[gains + 2 * layers : gains + 2 * layers + 1, block]
                    voice = voice + jnp.sum(fresh * wave, axis=1, keepdims=True)
            if i == layers - 1:
                out_ref[:, p : p + 1] = voice[BACK:, :]


def other_half(weight, axis):
    seg = lax.axis_index("segment")
    share = weight.shape[axis] // 2
    mine = lax.dynamic_slice_in_dim(weight, seg * share, share, axis)
    return swapped(mine, "mp")


def joined(share, axis):
    return lax.all_gather(share, "segment", axis=axis, tiled=True)


def route_kernel(per_device, offset_ref, ids_ref, *out_refs):
    steps, topk, wide = ids_ref.shape
    rows = wide // QUARTERS
    spread_ref = out_refs[-1]
    experts, columns = spread_ref.shape
    group = per_device * QUARTERS

    def iota(shape, axis):
        return lax.broadcasted_iota(jnp.int32, shape, axis)

    def ones(condition):
        return jnp.where(condition, 1.0, 0.0)

    name = iota((experts, wide), 0)
    ahead, behind = iota((wide, wide), 0), iota((wide, wide), 1)
    same = ahead // rows == behind // rows
    below = ones(same & (ahead % rows < behind % rows)).astype(BF16)
    unit = ones(iota((rows, wide), 0) == iota((rows, wide), 1)).astype(BF16)
    spread = ones(iota((experts, columns), 1) // group == iota((experts, columns), 0)).astype(BF16)
    tall = ones(iota((columns, experts), 0) // group == iota((columns, experts), 1)).astype(BF16)
    slot_row = iota((1, columns), 1) // QUARTERS % per_device
    column = iota((columns, wide), 0)
    slot_column = (column // QUARTERS % per_device).astype(F32)
    own = column % QUARTERS == iota((columns, wide), 1) // rows
    spread_ref[...] = spread
    for s in range(steps):
        hot_ref, mask_ref, pick_ref = out_refs[3 * s : 3 * s + 3]
        named = jnp.zeros((experts, wide), F32)
        for k in range(topk):
            named = named + ones(ids_ref[s, k : k + 1, :] == name)
        earlier = dot(named.astype(BF16), below)
        code = jnp.where(named > 0.0, earlier - offset_ref[0, 0], -64.0).astype(BF16)
        upright = dot_t(unit, code)
        hot_ref[...] = ones(upright > -32.0)
        mask_ref[...] = ones(dot(upright.astype(BF16), spread) == slot_row.astype(F32)).astype(BF16)
        pick_ref[...] = ones((dot(tall, code) == slot_column) & own).astype(BF16)


def on_device(
    start_state,
    expert_ids,
    norm_gain,
    w_router,
    w_gate,
    w_up,
    w_down,
    w_in,
    trans_taps,
    dw_kernels,
    ln_gain,
    ln_bias,
    w_out,
):
    seg = lax.axis_index("segment")
    mp = lax.axis_index("mp")
    rows, half = start_state.shape
    experts = w_router.shape[1]
    steps, _, topk = expert_ids.shape
    layers, kernel, channels = dw_kernels.shape
    channels = 2 * channels
    capacity = min(rows, max(2, 2 * rows * topk // experts))
    per_device = capacity // 4
    slots = experts * per_device
    offset = ((mp * 2 + seg) * per_device).astype(F32)
    depth = 2 * half
    width = depth // QUARTERS
    share = 2 * rows

    def ordered(mine, other, axis):
        return jnp.where(
            mp == 0,
            jnp.concatenate([mine, other], axis=axis),
            jnp.concatenate([other, mine], axis=axis),
        )

    gate, up, down = w_gate[0].T, w_up[0].T, w_down[0]
    part = gate.shape[0] // 2
    top = rows // 2
    packed, head = call(
        pack_kernel,
        (HBM((top + BACK + 3 * part, depth), BF16), HBM((top + BACK, depth), BF16)),
        seg.astype(jnp.int32).reshape(1, 1),
        start_state,
        norm_gain[None],
        gate,
        up,
        down,
        scratch=[
            pltpu.VMEM((top + BACK, depth), BF16),
            pltpu.SemaphoreType.DMA((5,)),
        ],
        places=[SMEM, VMEM, VMEM, HBM, HBM, HBM],
        grant=60,
    )
    sent = swapped(packed, "mp")
    x, gain = call(
        unpack_kernel,
        (shaped((QUARTERS * rows, width), BF16), shaped((QUARTERS, width), F32)),
        mp.astype(jnp.int32).reshape(1, 1),
        head,
        sent[: top + BACK],
        places=[SMEM, VMEM, VMEM],
    )
    gate_share, up_share, down_share = (
        sent[top + BACK + i * part : top + BACK + (i + 1) * part] for i in range(3)
    )
    small = jnp.concatenate(
        [trans_taps, dw_kernels.reshape(layers * kernel, -1), ln_gain, ln_bias, w_out[None]], axis=0
    )
    small = jnp.concatenate([small, voiced_swap(small)], axis=1)
    router_share = other_half(w_router, 0)
    keep = jnp.where(lax.axis_index("rows") == 0, 0.0, 1.0).astype(F32).reshape(1, 1)

    turned = expert_ids.transpose(0, 2, 1)
    columns = slots * QUARTERS
    made = call(
        functools.partial(route_kernel, per_device),
        [
            shaped((rows, experts), F32),
            shaped((rows, columns), BF16),
            shaped((columns, QUARTERS * rows), BF16),
        ]
        * steps
        + [shaped((experts, columns), BF16)],
        offset.reshape(1, 1),
        jnp.concatenate([turned] * QUARTERS, axis=2),
        grant=16,
        flops=4 * steps * columns * experts * QUARTERS * rows,
    )
    spread = made[-1]
    hots, masks, picks = made[:-1:3], made[1:-1:3], made[2:-1:3]
    gate2 = up2 = down2 = router = None
    frames = None
    voiced = []

    def voice(frames):
        return call(
            functools.partial(vocoder_kernel, layers, kernel),
            shaped((rows, 2), F32),
            keep,
            frames,
            small,
            scratch=[
                pltpu.VMEM((2, rows + BACK, channels), F32),
                pltpu.VMEM((2, rows + BACK, channels), F32),
            ],
            flops=20 * rows * channels * kernel,
        )

    for step in range(steps):
        hot, mask, pick = hots[step], masks[step], picks[step]
        outgoing, normed = call(
            functools.partial(norm_kernel, depth),
            (HBM((slots * QUARTERS, width), BF16), HBM((QUARTERS * rows, width), BF16)),
            x,
            gain,
            pick,
            scratch=[
                pltpu.VMEM((QUARTERS * rows, width), BF16),
                pltpu.VMEM((QUARTERS, slots, width), BF16),
                pltpu.SemaphoreType.DMA((QUARTERS + 1,)),
            ],
            flops=2 * slots * QUARTERS * QUARTERS * rows * width,
        )
        received = lax.all_to_all(
            outgoing.reshape(experts, per_device * QUARTERS, width),
            "rows",
            split_axis=0,
            concat_axis=0,
            tiled=True,
        )
        if step == 0:
            gate2, up2, down2 = joined(gate_share, 0), joined(up_share, 0), joined(down_share, 0)
            router = ordered(w_router, joined(router_share, 0), 0)
        weights = call(
            weight_kernel,
            shaped((2 * rows, slots * QUARTERS), BF16),
            normed,
            router,
            hot,
            spread,
            mask,
            flops=4 * rows * experts * (depth + slots * QUARTERS),
        )
        if frames is not None:
            received, frames, weights = lax.optimization_barrier((received, frames, weights))
        answer = call(
            expert_kernel,
            HBM((slots * QUARTERS, width), BF16),
            received.reshape(slots * QUARTERS, width),
            gate,
            gate2,
            up,
            up2,
            down,
            down2,
            scratch=[
                pltpu.VMEM((width // LANES, slots * QUARTERS, LANES), F32),
                pltpu.VMEM((QUARTERS, slots, width), BF16),
                pltpu.SemaphoreType.DMA((QUARTERS,)),
            ],
            grant=12,
            flops=12 * slots * depth * w_gate.shape[2],
        )
        back = lax.all_to_all(
            answer.reshape(experts, per_device * QUARTERS, width),
            "rows",
            split_axis=0,
            concat_axis=0,
            tiled=True,
        )
        if frames is not None:
            sound = voice(frames)
            back, sound = lax.optimization_barrier((back, sound))
            voiced.append(sound)
        partial = call(
            combine_kernel,
            shaped((QUARTERS * rows, width), BF16),
            weights,
            back.reshape(slots * QUARTERS, width),
            flops=4 * slots * QUARTERS * QUARTERS * rows * width,
        )
        chip = lax.all_gather(partial, "segment", axis=0)
        chip = lax.dynamic_slice_in_dim(chip, seg * share, share, 1).astype(F32)
        chip = (chip[0] + chip[1]).astype(BF16)
        total = lax.all_gather(chip, "mp", axis=0).astype(F32)
        mine = lax.dynamic_slice_in_dim(x, seg * share, share, 0).astype(F32)
        fresh = (mine + (total[0] + total[1])).astype(BF16)
        x = lax.all_gather(fresh, "segment", axis=0, tiled=True)

        own = sum(
            dot(x[q * rows : (q + 1) * rows], w_in[q * width : (q + 1) * width])
            for q in range(QUARTERS)
        ).astype(BF16)
        frames = jnp.concatenate([own, voiced_swap(own)], axis=1)
        frames = jnp.concatenate([voiced_pass(frames[-BACK:]), frames], axis=0)
    voiced.append(voice(frames))
    audio = jnp.stack([v.reshape(2 * rows) for v in voiced], axis=0)
    audio = jnp.where(seg == 0, jnp.zeros_like(audio), audio)[None]
    state = lax.dynamic_slice_in_dim(x, mp * share, share, 0)
    state = jnp.concatenate([state[:rows], state[rows:]], axis=1)
    return state, audio


def solution(mesh):
    return jax.shard_map(
        on_device,
        mesh=mesh,
        in_specs=(
            P("rows", "mp"),
            P(None, "rows", None),
            P("mp"),
            P("mp", None),
            P("rows", None, "mp"),
            P("rows", None, "mp"),
            P("rows", "mp", None),
            P(None, "mp"),
            P(None, "mp"),
            P(None, None, "mp"),
            P(None, "mp"),
            P(None, "mp"),
            P("mp"),
        ),
        out_specs=(P("rows", "mp"), P("segment", None, "rows")),
        check_vma=False,
    )
```

```python
import functools
import math

import jax
import jax.numpy as jnp
from jax import lax
from jax.experimental import pallas as pl
from jax.experimental.pallas import tpu as pltpu
from jax.sharding import PartitionSpec as P

BF16 = jnp.bfloat16
F32 = jnp.float32
QUARTERS = 4
BACK = 16
LANES = 128
VMEM = pltpu.VMEM
SMEM = pltpu.SMEM
HBM = pltpu.HBM


def dot(a, b):
    return jnp.dot(a, b, preferred_element_type=F32)


def dot_t(a, b):
    return lax.dot_general(a, b, (((1,), (1,)), ((), ())), preferred_element_type=F32)


def swapped(block, axis):
    return lax.ppermute(block, axis, [(0, 1), (1, 0)])


def voiced_swap(block):
    return lax.ppermute(block, ("segment", "mp"), [(2, 3), (3, 2)])


def voiced_pass(block, across):
    count = lax.axis_size("rows")
    route = [
        (2 * (count + i) + m, 2 * (count + i + 1) + (m ^ across))
        for i in range(count - 1)
        for m in range(2)
    ]
    return lax.ppermute(block, ("segment", "rows", "mp"), route)


def call(kernel, outs, *args, scratch=(), flops=0, places=None, grant=10):
    single = not isinstance(outs, (list, tuple))
    listed = [outs] if single else list(outs)
    moved = sum(math.prod(a.shape) * a.dtype.itemsize for a in list(args) + listed)
    places = places or [VMEM] * len(args)
    specs = [p if isinstance(p, pl.BlockSpec) else pl.BlockSpec(memory_space=p) for p in places]
    out_specs = [pl.BlockSpec(memory_space=getattr(o, "memory_space", VMEM)) for o in listed]
    out_specs = [
        s if s.memory_space in (VMEM, HBM) else pl.BlockSpec(memory_space=VMEM) for s in out_specs
    ]
    return pl.pallas_call(
        kernel,
        out_shape=outs,
        in_specs=specs,
        out_specs=out_specs[0] if single else out_specs,
        scratch_shapes=list(scratch),
        compiler_params=pltpu.CompilerParams(vmem_limit_bytes=grant * 1024 * 1024),
        cost_estimate=pl.CostEstimate(flops=flops, bytes_accessed=moved, transcendentals=0),
    )(*args)


def shaped(shape, dtype):
    return jax.ShapeDtypeStruct(shape, dtype)


def pack_kernel(
    seg_ref,
    state_ref,
    gain_ref,
    gate_ref,
    up_ref,
    down_ref,
    out_ref,
    head_out,
    head_ref,
    part_ref,
    sems,
):
    rows, half = state_ref.shape
    top = rows // 2
    share = gate_ref.shape[0] // 2
    from_row = pl.multiple_of(seg_ref[0, 0] * share, share)
    loads = []
    for i, ref in enumerate((gate_ref, up_ref, down_ref)):
        load = pltpu.make_async_copy(
            ref.at[pl.ds(from_row, share), :], part_ref.at[i], sems.at[i]
        )
        load.start()
        loads.append(load)
    head_ref[:top, :half] = state_ref[:top, :]
    head_ref[:top, half:] = state_ref[top:, :]
    gain = gain_ref[...]
    high = gain.astype(BF16)
    rest = gain - high.astype(F32)
    middle = rest.astype(BF16)
    low = (rest - middle.astype(F32)).astype(BF16)
    row = lax.broadcasted_iota(jnp.int32, (BACK, half), 0)
    terms = jnp.zeros((BACK, half), F32)
    for i, term in enumerate((high, middle, low)):
        terms = jnp.where(row == i, term.astype(F32), terms)
    head_ref[top:, :half] = terms.astype(BF16)
    head_ref[top:, half:] = terms.astype(BF16)
    copies = [
        pltpu.make_async_copy(head_ref, out_ref.at[pl.ds(0, top + BACK), :], sems.at[3]),
        pltpu.make_async_copy(head_ref, head_out, sems.at[4]),
    ]
    for copy in copies:
        copy.start()
    for i, load in enumerate(loads):
        load.wait()
        place = top + BACK + i * share
        copy = pltpu.make_async_copy(
            part_ref.at[i], out_ref.at[pl.ds(place, share), :], sems.at[5 + i]
        )
        copy.start()
        copies.append(copy)
    for copy in copies:
        copy.wait()


def unpack_kernel(mp_ref, mine_ref, other_ref, x_ref, gain_ref):
    rows = x_ref.shape[0] // QUARTERS
    width = x_ref.shape[1]
    top = rows // 2
    ours = mp_ref[0, 0]
    for h in range(2):
        for q in range(2):
            for r in range(2):
                columns = slice((2 * r + q) * width, (2 * r + q + 1) * width)
                start = (2 * h + q) * rows + r * top
                mine = mine_ref[:top, columns].astype(F32)
                other = other_ref[:top, columns].astype(F32)
                x_ref[start : start + top, :] = jnp.where(ours == h, mine, other).astype(BF16)
            columns = slice(q * width, (q + 1) * width)
            mine = mine_ref[top : top + BACK, columns].astype(F32)
            other = other_ref[top : top + BACK, columns].astype(F32)
            terms = jnp.where(ours == h, mine, other)
            gain_ref[2 * h + q : 2 * h + q + 1, :] = (terms[0:1] + terms[1:2]) + terms[2:3]


def norm_kernel(depth, x_ref, gain_ref, pick_ref, out_ref, normed_out, normed_ref, held_ref, sems):
    rows = x_ref.shape[0] // QUARTERS
    total = jnp.zeros((rows, 1), F32)
    for q in range(QUARTERS):
        part = x_ref[q * rows : (q + 1) * rows, :].astype(F32)
        total = total + jnp.sum(part * part, axis=1, keepdims=True)
    scale = lax.rsqrt(total / depth + 1e-06)
    for q in range(QUARTERS):
        part = x_ref[q * rows : (q + 1) * rows, :].astype(F32)
        normed_ref[q * rows : (q + 1) * rows, :] = (
            part * scale * gain_ref[q : q + 1, :]
        ).astype(BF16)
    copies = [pltpu.make_async_copy(normed_ref, normed_out, sems.at[QUARTERS])]
    copies[0].start()
    normed = normed_ref[...]
    size = pick_ref.shape[0] // QUARTERS
    for i in range(QUARTERS):
        held_ref[i] = dot(pick_ref[i * size : (i + 1) * size, :], normed).astype(BF16)
        copy = pltpu.make_async_copy(
            held_ref.at[i], out_ref.at[pl.ds(i * size, size), :], sems.at[i]
        )
        copy.start()
        copies.append(copy)
    for copy in copies:
        copy.wait()


def weight_kernel(normed_ref, router_ref, hot_ref, spread_ref, mask_ref, out_ref):
    rows = normed_ref.shape[0] // QUARTERS
    width = normed_ref.shape[1]
    logits = jnp.zeros(hot_ref.shape, F32)
    for q in range(QUARTERS):
        logits = logits + dot(
            normed_ref[q * rows : (q + 1) * rows, :], router_ref[q * width : (q + 1) * width, :]
        )
    squashed = jnp.where(hot_ref[...] > 0.0, jax.nn.sigmoid(logits), 0.0)
    weights = squashed / jnp.sum(squashed, axis=1, keepdims=True)
    high = weights.astype(BF16)
    low = (weights - high.astype(F32)).astype(BF16)
    mask = mask_ref[...].astype(F32)
    out_ref[:rows, :] = (dot(high, spread_ref[...]) * mask).astype(BF16)
    out_ref[rows:, :] = (dot(low, spread_ref[...]) * mask).astype(BF16)


def expert_kernel(
    in_ref,
    gate_ref,
    gate2_ref,
    up_ref,
    up2_ref,
    down_ref,
    down2_ref,
    out_ref,
    wide_ref,
    answer_ref,
    sems,
):
    count, width = in_ref.shape
    slots = count // QUARTERS
    lanes = gate_ref.shape[0]
    pieces = width // LANES
    for c in range(pieces):
        wide_ref[c] = in_ref[:, c * LANES : (c + 1) * LANES].astype(F32)
    sums = [jnp.zeros((slots, lanes), F32) for _ in range(4)]
    for q in range(QUARTERS):
        part = jnp.concatenate(
            [wide_ref[c, pl.ds(q, slots, stride=QUARTERS), :] for c in range(pieces)], axis=1
        ).astype(BF16)
        columns = slice(q * width, (q + 1) * width)
        for i, ref in enumerate((gate_ref, gate2_ref, up_ref, up2_ref)):
            sums[i] = sums[i] + dot_t(part, ref[:, columns])
    first = (sums[0] / (1.0 + jnp.exp(-sums[0])) * sums[2]).astype(BF16)
    second = (sums[1] / (1.0 + jnp.exp(-sums[1])) * sums[3]).astype(BF16)
    for q in range(QUARTERS):
        columns = slice(q * width, (q + 1) * width)
        answer = dot(first, down_ref[:, columns]) + dot(second, down2_ref[:, columns])
        for c in range(pieces):
            wide_ref[c, pl.ds(q, slots, stride=QUARTERS), :] = answer[:, c * LANES : (c + 1) * LANES]
    stores = []
    size = count // QUARTERS
    for i in range(QUARTERS):
        span = slice(i * size, (i + 1) * size)
        for c in range(pieces):
            answer_ref[i, :, c * LANES : (c + 1) * LANES] = wide_ref[c, span, :].astype(BF16)
        store = pltpu.make_async_copy(
            answer_ref.at[i], out_ref.at[pl.ds(i * size, size), :], sems.at[i]
        )
        store.start()
        stores.append(store)
    for store in stores:
        store.wait()


def combine_kernel(weight_ref, back_ref, out_ref):
    rows = weight_ref.shape[0] // 2
    weights = weight_ref[...].astype(F32)
    lane = lax.broadcasted_iota(jnp.int32, weights.shape, 1) % QUARTERS
    chosen = jnp.concatenate(
        [jnp.where(lane == q, weights, 0.0).astype(BF16) for q in range(QUARTERS)], axis=0
    )
    mixed = dot(chosen, back_ref[...])
    for q in range(QUARTERS):
        start = 2 * q * rows
        out_ref[q * rows : (q + 1) * rows, :] = (
            mixed[start : start + rows] + mixed[start + rows : start + 2 * rows]
        ).astype(BF16)


def vocoder_kernel(layers, kernel, keep_ref, frame_ref, small_ref, out_ref, phase_ref, mixed_ref):
    count, channels = frame_ref.shape
    chunk = 256
    gains = 4 + layers * kernel
    blocks = [slice(c, c + chunk) for c in range(0, channels, chunk)]

    def back(value, frames):
        return value if frames == 0 else pltpu.roll(value, frames, 0)

    row = lax.broadcasted_iota(jnp.int32, (count, 1), 0)
    live = jnp.where(row < BACK, keep_ref[0, 0], 1.0)
    for block in blocks:
        now = frame_ref[:, block].astype(F32)
        before = back(now, 1)
        for p in range(2):
            phase_ref[p, :, block] = (
                small_ref[p : p + 1, block] * now + small_ref[p + 2 : p + 3, block] * before
            ).astype(BF16).astype(F32)
    for i in range(layers):
        dilation = 3**i
        sums = [jnp.zeros((count, 1), F32) for _ in range(2)]
        powers = [jnp.zeros((count, 1), F32) for _ in range(2)]
        for block in blocks:
            phases = [phase_ref[0, :, block], phase_ref[1, :, block]]
            for p in range(2):
                mixed = jnp.zeros((count, chunk), F32)
                for j in range(kernel):
                    at = p - j * dilation
                    tap = small_ref[4 + i * kernel + j : 5 + i * kernel + j, block]
                    mixed = mixed + tap * back(phases[at % 2], -(at // 2))
                mixed_ref[p, :, block] = mixed
                sums[p] = sums[p] + jnp.sum(mixed, axis=1, keepdims=True)
                powers[p] = powers[p] + jnp.sum(mixed * mixed, axis=1, keepdims=True)
        for p in range(2):
            center = sums[p] / channels
            scale = lax.rsqrt(powers[p] / channels - center * center + 1e-06)
            voice = jnp.zeros((count, 1), F32)
            for block in blocks:
                gain = small_ref[gains + i : gains + i + 1, block]
                bias = small_ref[gains + layers + i : gains + layers + i + 1, block]
                fresh = (
                    phase_ref[p, :, block]
                    + (mixed_ref[p, :, block] - center) * scale * gain
                    + bias
                )
                fresh = fresh.astype(BF16).astype(F32)
                if i < layers - 1:
                    phase_ref[p, :, block] = fresh * live
                else:
                    wave = small_ref[gains + 2 * layers : gains + 2 * layers + 1, block]
                    voice = voice + jnp.sum(fresh * wave, axis=1, keepdims=True)
            if i == layers - 1:
                out_ref[:, p : p + 1] = voice[BACK:, :]


def other_half(weight, axis):
    seg = lax.axis_index("segment")
    share = weight.shape[axis] // 2
    mine = lax.dynamic_slice_in_dim(weight, seg * share, share, axis)
    return swapped(mine, "mp")


def joined(share, axis):
    return lax.all_gather(share, "segment", axis=axis, tiled=True)


def route_kernel(per_device, offset_ref, ids_ref, *out_refs):
    steps, topk, wide = ids_ref.shape
    rows = wide // QUARTERS
    spread_ref = out_refs[-1]
    experts, columns = spread_ref.shape
    group = per_device * QUARTERS

    def iota(shape, axis):
        return lax.broadcasted_iota(jnp.int32, shape, axis)

    def ones(condition):
        return jnp.where(condition, 1.0, 0.0)

    name = iota((experts, wide), 0)
    ahead, behind = iota((wide, wide), 0), iota((wide, wide), 1)
    same = ahead // rows == behind // rows
    below = ones(same & (ahead % rows < behind % rows)).astype(BF16)
    unit = ones(iota((rows, wide), 0) == iota((rows, wide), 1)).astype(BF16)
    spread = ones(iota((experts, columns), 1) // group == iota((experts, columns), 0)).astype(BF16)
    tall = ones(iota((columns, experts), 0) // group == iota((columns, experts), 1)).astype(BF16)
    slot_row = iota((1, columns), 1) // QUARTERS % per_device
    column = iota((columns, wide), 0)
    slot_column = (column // QUARTERS % per_device).astype(F32)
    own = column % QUARTERS == iota((columns, wide), 1) // rows
    spread_ref[...] = spread
    for s in range(steps):
        hot_ref, mask_ref, pick_ref = out_refs[3 * s : 3 * s + 3]
        named = jnp.zeros((experts, wide), F32)
        for k in range(topk):
            named = named + ones(ids_ref[s, k : k + 1, :] == name)
        earlier = dot(named.astype(BF16), below)
        code = jnp.where(named > 0.0, earlier - offset_ref[0, 0], -64.0).astype(BF16)
        upright = dot_t(unit, code)
        hot_ref[...] = ones(upright > -32.0)
        mask_ref[...] = ones(dot(upright.astype(BF16), spread) == slot_row.astype(F32)).astype(BF16)
        pick_ref[...] = ones((dot(tall, code) == slot_column) & own).astype(BF16)


def on_device(
    start_state,
    expert_ids,
    norm_gain,
    w_router,
    w_gate,
    w_up,
    w_down,
    w_in,
    trans_taps,
    dw_kernels,
    ln_gain,
    ln_bias,
    w_out,
):
    seg = lax.axis_index("segment")
    mp = lax.axis_index("mp")
    rows, half = start_state.shape
    experts = w_router.shape[1]
    steps, _, topk = expert_ids.shape
    layers, kernel, channels = dw_kernels.shape
    channels = 2 * channels
    capacity = min(rows, max(2, 2 * rows * topk // experts))
    per_device = capacity // 4
    slots = experts * per_device
    offset = ((mp * 2 + seg) * per_device).astype(F32)
    depth = 2 * half
    width = depth // QUARTERS
    share = 2 * rows

    def ordered(mine, other, axis):
        return jnp.where(
            mp == 0,
            jnp.concatenate([mine, other], axis=axis),
            jnp.concatenate([other, mine], axis=axis),
        )

    gate, up, down = w_gate[0].T, w_up[0].T, w_down[0]
    part = gate.shape[0] // 2
    top = rows // 2
    packed, head = call(
        pack_kernel,
        (HBM((top + BACK + 3 * part, depth), BF16), HBM((top + BACK, depth), BF16)),
        seg.astype(jnp.int32).reshape(1, 1),
        start_state,
        norm_gain[None],
        gate,
        up,
        down,
        scratch=[
            pltpu.VMEM((top + BACK, depth), BF16),
            pltpu.VMEM((3, part, depth), BF16),
            pltpu.SemaphoreType.DMA((8,)),
        ],
        places=[SMEM, VMEM, VMEM, HBM, HBM, HBM],
        grant=60,
    )
    sent = swapped(packed, "mp")
    x, gain = call(
        unpack_kernel,
        (shaped((QUARTERS * rows, width), BF16), shaped((QUARTERS, width), F32)),
        mp.astype(jnp.int32).reshape(1, 1),
        head,
        sent[: top + BACK],
        places=[SMEM, VMEM, VMEM],
    )
    gate_share, up_share, down_share = (
        sent[top + BACK + i * part : top + BACK + (i + 1) * part] for i in range(3)
    )
    small = jnp.concatenate(
        [trans_taps, dw_kernels.reshape(layers * kernel, -1), ln_gain, ln_bias, w_out[None]], axis=0
    )
    small = jnp.concatenate([small, voiced_swap(small)], axis=1)
    router_share = other_half(w_router, 0)
    keep = jnp.where(lax.axis_index("rows") == 0, 0.0, 1.0).astype(F32).reshape(1, 1)

    turned = expert_ids.transpose(0, 2, 1)
    columns = slots * QUARTERS
    made = call(
        functools.partial(route_kernel, per_device),
        [
            shaped((rows, experts), F32),
            shaped((rows, columns), BF16),
            shaped((columns, QUARTERS * rows), BF16),
        ]
        * steps
        + [shaped((experts, columns), BF16)],
        offset.reshape(1, 1),
        jnp.concatenate([turned] * QUARTERS, axis=2),
        grant=16,
        flops=4 * steps * columns * experts * QUARTERS * rows,
    )
    spread = made[-1]
    hots, masks, picks = made[:-1:3], made[1:-1:3], made[2:-1:3]
    gate2 = up2 = down2 = router = None
    frames = None
    voiced = []

    def voice(frames):
        return call(
            functools.partial(vocoder_kernel, layers, kernel),
            shaped((rows, 2), F32),
            keep,
            frames,
            small,
            scratch=[
                pltpu.VMEM((2, rows + BACK, channels), F32),
                pltpu.VMEM((2, rows + BACK, channels), F32),
            ],
            flops=20 * rows * channels * kernel,
        )

    for step in range(steps):
        hot, mask, pick = hots[step], masks[step], picks[step]
        outgoing, normed = call(
            functools.partial(norm_kernel, depth),
            (HBM((slots * QUARTERS, width), BF16), HBM((QUARTERS * rows, width), BF16)),
            x,
            gain,
            pick,
            scratch=[
                pltpu.VMEM((QUARTERS * rows, width), BF16),
                pltpu.VMEM((QUARTERS, slots, width), BF16),
                pltpu.SemaphoreType.DMA((QUARTERS + 1,)),
            ],
            flops=2 * slots * QUARTERS * QUARTERS * rows * width,
        )
        received = lax.all_to_all(
            outgoing.reshape(experts, per_device * QUARTERS, width),
            "rows",
            split_axis=0,
            concat_axis=0,
            tiled=True,
        )
        if step == 0:
            gate2, up2, down2 = joined(gate_share, 0), joined(up_share, 0), joined(down_share, 0)
            router = ordered(w_router, joined(router_share, 0), 0)
        weights = call(
            weight_kernel,
            shaped((2 * rows, slots * QUARTERS), BF16),
            normed,
            router,
            hot,
            spread,
            mask,
            flops=4 * rows * experts * (depth + slots * QUARTERS),
        )
        if frames is not None:
            received, frames, weights = lax.optimization_barrier((received, frames, weights))
        answer = call(
            expert_kernel,
            HBM((slots * QUARTERS, width), BF16),
            received.reshape(slots * QUARTERS, width),
            gate,
            gate2,
            up,
            up2,
            down,
            down2,
            scratch=[
                pltpu.VMEM((width // LANES, slots * QUARTERS, LANES), F32),
                pltpu.VMEM((QUARTERS, slots, width), BF16),
                pltpu.SemaphoreType.DMA((QUARTERS,)),
            ],
            grant=12,
            flops=12 * slots * depth * w_gate.shape[2],
        )
        back = lax.all_to_all(
            answer.reshape(experts, per_device * QUARTERS, width),
            "rows",
            split_axis=0,
            concat_axis=0,
            tiled=True,
        )
        if frames is not None:
            sound = voice(frames)
            back, sound = lax.optimization_barrier((back, sound))
            voiced.append(sound)
        partial = call(
            combine_kernel,
            shaped((QUARTERS * rows, width), BF16),
            weights,
            back.reshape(slots * QUARTERS, width),
            flops=4 * slots * QUARTERS * QUARTERS * rows * width,
        )
        chip = lax.all_gather(partial, "segment", axis=0)
        chip = lax.dynamic_slice_in_dim(chip, seg * share, share, 1).astype(F32)
        chip = (chip[0] + chip[1]).astype(BF16)
        total = lax.all_gather(chip, "mp", axis=0).astype(F32)
        mine = lax.dynamic_slice_in_dim(x, seg * share, share, 0).astype(F32)
        fresh = (mine + (total[0] + total[1])).astype(BF16)
        x = lax.all_gather(fresh, "segment", axis=0, tiled=True)

        own = sum(
            dot(x[q * rows : (q + 1) * rows], w_in[q * width : (q + 1) * width])
            for q in range(QUARTERS)
        ).astype(BF16)
        last = own[-BACK:]
        near = jnp.concatenate([voiced_pass(last, 0), own], axis=0)
        far = jnp.concatenate([voiced_pass(last, 1), voiced_swap(own)], axis=0)
        frames = jnp.concatenate([near, far], axis=1)
    voiced.append(voice(frames))
    audio = jnp.stack([v.reshape(2 * rows) for v in voiced], axis=0)
    audio = jnp.where(seg == 0, jnp.zeros_like(audio), audio)[None]
    state = lax.dynamic_slice_in_dim(x, mp * share, share, 0)
    state = jnp.concatenate([state[:rows], state[rows:]], axis=1)
    return state, audio


def solution(mesh):
    return jax.shard_map(
        on_device,
        mesh=mesh,
        in_specs=(
            P("rows", "mp"),
            P(None, "rows", None),
            P("mp"),
            P("mp", None),
            P("rows", None, "mp"),
            P("rows", None, "mp"),
            P("rows", "mp", None),
            P(None, "mp"),
            P(None, "mp"),
            P(None, None, "mp"),
            P(None, "mp"),
            P(None, "mp"),
            P("mp"),
        ),
        out_specs=(P("rows", "mp"), P("segment", None, "rows")),
        check_vma=False,
    )
```

```python
import functools
import math

import jax
import jax.numpy as jnp
from jax import lax
from jax.experimental import pallas as pl
from jax.experimental.pallas import tpu as pltpu
from jax.sharding import PartitionSpec as P

BF16 = jnp.bfloat16
F32 = jnp.float32
QUARTERS = 4
BACK = 16
LANES = 128
VMEM = pltpu.VMEM
SMEM = pltpu.SMEM
HBM = pltpu.HBM


def dot(a, b):
    return jnp.dot(a, b, preferred_element_type=F32)


def dot_t(a, b):
    return lax.dot_general(a, b, (((1,), (1,)), ((), ())), preferred_element_type=F32)


def swapped(block, axis):
    return lax.ppermute(block, axis, [(0, 1), (1, 0)])


def voiced_swap(block):
    return lax.ppermute(block, ("segment", "mp"), [(2, 3), (3, 2)])


def voiced_pass(block, across):
    count = lax.axis_size("rows")
    route = [
        (2 * (count + i) + m, 2 * (count + i + 1) + (m ^ across))
        for i in range(count - 1)
        for m in range(2)
    ]
    return lax.ppermute(block, ("segment", "rows", "mp"), route)


def call(kernel, outs, *args, scratch=(), flops=0, places=None, grant=10):
    single = not isinstance(outs, (list, tuple))
    listed = [outs] if single else list(outs)
    moved = sum(math.prod(a.shape) * a.dtype.itemsize for a in list(args) + listed)
    places = places or [VMEM] * len(args)
    specs = [p if isinstance(p, pl.BlockSpec) else pl.BlockSpec(memory_space=p) for p in places]
    out_specs = [pl.BlockSpec(memory_space=getattr(o, "memory_space", VMEM)) for o in listed]
    out_specs = [
        s if s.memory_space in (VMEM, HBM) else pl.BlockSpec(memory_space=VMEM) for s in out_specs
    ]
    return pl.pallas_call(
        kernel,
        out_shape=outs,
        in_specs=specs,
        out_specs=out_specs[0] if single else out_specs,
        scratch_shapes=list(scratch),
        compiler_params=pltpu.CompilerParams(vmem_limit_bytes=grant * 1024 * 1024),
        cost_estimate=pl.CostEstimate(flops=flops, bytes_accessed=moved, transcendentals=0),
    )(*args)


def shaped(shape, dtype):
    return jax.ShapeDtypeStruct(shape, dtype)


def pack_kernel(
    seg_ref,
    state_ref,
    gain_ref,
    gate_ref,
    up_ref,
    down_ref,
    out_ref,
    head_out,
    head_ref,
    part_ref,
    sems,
):
    rows, half = state_ref.shape
    top = rows // 2
    share = gate_ref.shape[0] // 2
    from_row = pl.multiple_of(seg_ref[0, 0] * share, share)
    loads = []
    for i, ref in enumerate((gate_ref, up_ref, down_ref)):
        load = pltpu.make_async_copy(
            ref.at[pl.ds(from_row, share), :], part_ref.at[i], sems.at[i]
        )
        load.start()
        loads.append(load)
    head_ref[:top, :half] = state_ref[:top, :]
    head_ref[:top, half:] = state_ref[top:, :]
    gain = gain_ref[...]
    high = gain.astype(BF16)
    rest = gain - high.astype(F32)
    middle = rest.astype(BF16)
    low = (rest - middle.astype(F32)).astype(BF16)
    row = lax.broadcasted_iota(jnp.int32, (BACK, half), 0)
    terms = jnp.zeros((BACK, half), F32)
    for i, term in enumerate((high, middle, low)):
        terms = jnp.where(row == i, term.astype(F32), terms)
    head_ref[top:, :half] = terms.astype(BF16)
    head_ref[top:, half:] = terms.astype(BF16)
    copies = [
        pltpu.make_async_copy(head_ref, head_out, sems.at[3]),
    ]
    for copy in copies:
        copy.start()
    for i, load in enumerate(loads):
        load.wait()
        copy = pltpu.make_async_copy(
            part_ref.at[i], out_ref.at[pl.ds(i * share, share), :], sems.at[4 + i]
        )
        copy.start()
        copies.append(copy)
    for copy in copies:
        copy.wait()


def unpack_kernel(mp_ref, mine_ref, other_ref, x_ref, gain_ref):
    rows = x_ref.shape[0] // QUARTERS
    width = x_ref.shape[1]
    top = rows // 2
    ours = mp_ref[0, 0]
    for h in range(2):
        for q in range(2):
            for r in range(2):
                columns = slice((2 * r + q) * width, (2 * r + q + 1) * width)
                start = (2 * h + q) * rows + r * top
                mine = mine_ref[:top, columns].astype(F32)
                other = other_ref[:top, columns].astype(F32)
                x_ref[start : start + top, :] = jnp.where(ours == h, mine, other).astype(BF16)
            columns = slice(q * width, (q + 1) * width)
            mine = mine_ref[top : top + BACK, columns].astype(F32)
            other = other_ref[top : top + BACK, columns].astype(F32)
            terms = jnp.where(ours == h, mine, other)
            gain_ref[2 * h + q : 2 * h + q + 1, :] = (terms[0:1] + terms[1:2]) + terms[2:3]


def norm_kernel(depth, x_ref, gain_ref, pick_ref, out_ref, normed_out, normed_ref, held_ref, sems):
    rows = x_ref.shape[0] // QUARTERS
    total = jnp.zeros((rows, 1), F32)
    for q in range(QUARTERS):
        part = x_ref[q * rows : (q + 1) * rows, :].astype(F32)
        total = total + jnp.sum(part * part, axis=1, keepdims=True)
    scale = lax.rsqrt(total / depth + 1e-06)
    for q in range(QUARTERS):
        part = x_ref[q * rows : (q + 1) * rows, :].astype(F32)
        normed_ref[q * rows : (q + 1) * rows, :] = (
            part * scale * gain_ref[q : q + 1, :]
        ).astype(BF16)
    copies = [pltpu.make_async_copy(normed_ref, normed_out, sems.at[QUARTERS])]
    copies[0].start()
    normed = normed_ref[...]
    size = pick_ref.shape[0] // QUARTERS
    for i in range(QUARTERS):
        held_ref[i] = dot(pick_ref[i * size : (i + 1) * size, :], normed).astype(BF16)
        copy = pltpu.make_async_copy(
            held_ref.at[i], out_ref.at[pl.ds(i * size, size), :], sems.at[i]
        )
        copy.start()
        copies.append(copy)
    for copy in copies:
        copy.wait()


def weight_kernel(normed_ref, router_ref, hot_ref, spread_ref, mask_ref, out_ref):
    rows = normed_ref.shape[0] // QUARTERS
    width = normed_ref.shape[1]
    logits = jnp.zeros(hot_ref.shape, F32)
    for q in range(QUARTERS):
        logits = logits + dot(
            normed_ref[q * rows : (q + 1) * rows, :], router_ref[q * width : (q + 1) * width, :]
        )
    squashed = jnp.where(hot_ref[...] > 0.0, jax.nn.sigmoid(logits), 0.0)
    weights = squashed / jnp.sum(squashed, axis=1, keepdims=True)
    high = weights.astype(BF16)
    low = (weights - high.astype(F32)).astype(BF16)
    mask = mask_ref[...].astype(F32)
    out_ref[:rows, :] = (dot(high, spread_ref[...]) * mask).astype(BF16)
    out_ref[rows:, :] = (dot(low, spread_ref[...]) * mask).astype(BF16)


def expert_kernel(
    in_ref,
    gate_ref,
    gate2_ref,
    up_ref,
    up2_ref,
    down_ref,
    down2_ref,
    out_ref,
    wide_ref,
    answer_ref,
    sems,
):
    count, width = in_ref.shape
    slots = count // QUARTERS
    lanes = gate_ref.shape[0]
    pieces = width // LANES
    for c in range(pieces):
        wide_ref[c] = in_ref[:, c * LANES : (c + 1) * LANES].astype(F32)
    sums = [jnp.zeros((slots, lanes), F32) for _ in range(4)]
    for q in range(QUARTERS):
        part = jnp.concatenate(
            [wide_ref[c, pl.ds(q, slots, stride=QUARTERS), :] for c in range(pieces)], axis=1
        ).astype(BF16)
        columns = slice(q * width, (q + 1) * width)
        for i, ref in enumerate((gate_ref, gate2_ref, up_ref, up2_ref)):
            sums[i] = sums[i] + dot_t(part, ref[:, columns])
    first = (sums[0] / (1.0 + jnp.exp(-sums[0])) * sums[2]).astype(BF16)
    second = (sums[1] / (1.0 + jnp.exp(-sums[1])) * sums[3]).astype(BF16)
    for q in range(QUARTERS):
        columns = slice(q * width, (q + 1) * width)
        answer = dot(first, down_ref[:, columns]) + dot(second, down2_ref[:, columns])
        for c in range(pieces):
            wide_ref[c, pl.ds(q, slots, stride=QUARTERS), :] = answer[:, c * LANES : (c + 1) * LANES]
    stores = []
    size = count // QUARTERS
    for i in range(QUARTERS):
        span = slice(i * size, (i + 1) * size)
        for c in range(pieces):
            answer_ref[i, :, c * LANES : (c + 1) * LANES] = wide_ref[c, span, :].astype(BF16)
        store = pltpu.make_async_copy(
            answer_ref.at[i], out_ref.at[pl.ds(i * size, size), :], sems.at[i]
        )
        store.start()
        stores.append(store)
    for store in stores:
        store.wait()


def combine_kernel(weight_ref, back_ref, out_ref):
    rows = weight_ref.shape[0] // 2
    weights = weight_ref[...].astype(F32)
    lane = lax.broadcasted_iota(jnp.int32, weights.shape, 1) % QUARTERS
    chosen = jnp.concatenate(
        [jnp.where(lane == q, weights, 0.0).astype(BF16) for q in range(QUARTERS)], axis=0
    )
    mixed = dot(chosen, back_ref[...])
    for q in range(QUARTERS):
        start = 2 * q * rows
        out_ref[q * rows : (q + 1) * rows, :] = (
            mixed[start : start + rows] + mixed[start + rows : start + 2 * rows]
        ).astype(BF16)


def vocoder_kernel(layers, kernel, keep_ref, frame_ref, small_ref, out_ref, phase_ref, mixed_ref):
    count, channels = frame_ref.shape
    chunk = 256
    gains = 4 + layers * kernel
    blocks = [slice(c, c + chunk) for c in range(0, channels, chunk)]

    def back(value, frames):
        return value if frames == 0 else pltpu.roll(value, frames, 0)

    row = lax.broadcasted_iota(jnp.int32, (count, 1), 0)
    live = jnp.where(row < BACK, keep_ref[0, 0], 1.0)
    for block in blocks:
        now = frame_ref[:, block].astype(F32)
        before = back(now, 1)
        for p in range(2):
            phase_ref[p, :, block] = (
                small_ref[p : p + 1, block] * now + small_ref[p + 2 : p + 3, block] * before
            ).astype(BF16).astype(F32)
    for i in range(layers):
        dilation = 3**i
        sums = [jnp.zeros((count, 1), F32) for _ in range(2)]
        powers = [jnp.zeros((count, 1), F32) for _ in range(2)]
        for block in blocks:
            phases = [phase_ref[0, :, block], phase_ref[1, :, block]]
            for p in range(2):
                mixed = jnp.zeros((count, chunk), F32)
                for j in range(kernel):
                    at = p - j * dilation
                    tap = small_ref[4 + i * kernel + j : 5 + i * kernel + j, block]
                    mixed = mixed + tap * back(phases[at % 2], -(at // 2))
                mixed_ref[p, :, block] = mixed
                sums[p] = sums[p] + jnp.sum(mixed, axis=1, keepdims=True)
                powers[p] = powers[p] + jnp.sum(mixed * mixed, axis=1, keepdims=True)
        for p in range(2):
            center = sums[p] / channels
            scale = lax.rsqrt(powers[p] / channels - center * center + 1e-06)
            voice = jnp.zeros((count, 1), F32)
            for block in blocks:
                gain = small_ref[gains + i : gains + i + 1, block]
                bias = small_ref[gains + layers + i : gains + layers + i + 1, block]
                fresh = (
                    phase_ref[p, :, block]
                    + (mixed_ref[p, :, block] - center) * scale * gain
                    + bias
                )
                fresh = fresh.astype(BF16).astype(F32)
                if i < layers - 1:
                    phase_ref[p, :, block] = fresh * live
                else:
                    wave = small_ref[gains + 2 * layers : gains + 2 * layers + 1, block]
                    voice = voice + jnp.sum(fresh * wave, axis=1, keepdims=True)
            if i == layers - 1:
                out_ref[:, p : p + 1] = voice[BACK:, :]


def other_half(weight, axis):
    seg = lax.axis_index("segment")
    share = weight.shape[axis] // 2
    mine = lax.dynamic_slice_in_dim(weight, seg * share, share, axis)
    return swapped(mine, "mp")


def joined(share, axis):
    return lax.all_gather(share, "segment", axis=axis, tiled=True)


def route_kernel(per_device, offset_ref, ids_ref, *out_refs):
    steps, topk, wide = ids_ref.shape
    rows = wide // QUARTERS
    spread_ref = out_refs[-1]
    experts, columns = spread_ref.shape
    group = per_device * QUARTERS

    def iota(shape, axis):
        return lax.broadcasted_iota(jnp.int32, shape, axis)

    def ones(condition):
        return jnp.where(condition, 1.0, 0.0)

    name = iota((experts, wide), 0)
    ahead, behind = iota((wide, wide), 0), iota((wide, wide), 1)
    same = ahead // rows == behind // rows
    below = ones(same & (ahead % rows < behind % rows)).astype(BF16)
    unit = ones(iota((rows, wide), 0) == iota((rows, wide), 1)).astype(BF16)
    spread = ones(iota((experts, columns), 1) // group == iota((experts, columns), 0)).astype(BF16)
    tall = ones(iota((columns, experts), 0) // group == iota((columns, experts), 1)).astype(BF16)
    slot_row = iota((1, columns), 1) // QUARTERS % per_device
    column = iota((columns, wide), 0)
    slot_column = (column // QUARTERS % per_device).astype(F32)
    own = column % QUARTERS == iota((columns, wide), 1) // rows
    spread_ref[...] = spread
    for s in range(steps):
        hot_ref, mask_ref, pick_ref = out_refs[3 * s : 3 * s + 3]
        named = jnp.zeros((experts, wide), F32)
        for k in range(topk):
            named = named + ones(ids_ref[s, k : k + 1, :] == name)
        earlier = dot(named.astype(BF16), below)
        code = jnp.where(named > 0.0, earlier - offset_ref[0, 0], -64.0).astype(BF16)
        upright = dot_t(unit, code)
        hot_ref[...] = ones(upright > -32.0)
        mask_ref[...] = ones(dot(upright.astype(BF16), spread) == slot_row.astype(F32)).astype(BF16)
        pick_ref[...] = ones((dot(tall, code) == slot_column) & own).astype(BF16)


def on_device(
    start_state,
    expert_ids,
    norm_gain,
    w_router,
    w_gate,
    w_up,
    w_down,
    w_in,
    trans_taps,
    dw_kernels,
    ln_gain,
    ln_bias,
    w_out,
):
    seg = lax.axis_index("segment")
    mp = lax.axis_index("mp")
    rows, half = start_state.shape
    experts = w_router.shape[1]
    steps, _, topk = expert_ids.shape
    layers, kernel, channels = dw_kernels.shape
    channels = 2 * channels
    capacity = min(rows, max(2, 2 * rows * topk // experts))
    per_device = capacity // 4
    slots = experts * per_device
    offset = ((mp * 2 + seg) * per_device).astype(F32)
    depth = 2 * half
    width = depth // QUARTERS
    share = 2 * rows

    def ordered(mine, other, axis):
        return jnp.where(
            mp == 0,
            jnp.concatenate([mine, other], axis=axis),
            jnp.concatenate([other, mine], axis=axis),
        )

    gate, up, down = w_gate[0].T, w_up[0].T, w_down[0]
    part = gate.shape[0] // 2
    top = rows // 2
    packed, head = call(
        pack_kernel,
        (HBM((3 * part, depth), BF16), HBM((top + BACK, depth), BF16)),
        seg.astype(jnp.int32).reshape(1, 1),
        start_state,
        norm_gain[None],
        gate,
        up,
        down,
        scratch=[
            pltpu.VMEM((top + BACK, depth), BF16),
            pltpu.VMEM((3, part, depth), BF16),
            pltpu.SemaphoreType.DMA((7,)),
        ],
        places=[SMEM, VMEM, VMEM, HBM, HBM, HBM],
        grant=60,
    )
    head_sent = swapped(head, "mp")
    sent = swapped(packed, "mp")
    x, gain = call(
        unpack_kernel,
        (shaped((QUARTERS * rows, width), BF16), shaped((QUARTERS, width), F32)),
        mp.astype(jnp.int32).reshape(1, 1),
        head,
        head_sent,
        places=[SMEM, VMEM, VMEM],
    )
    gate_share, up_share, down_share = (
        sent[i * part : (i + 1) * part] for i in range(3)
    )
    small = jnp.concatenate(
        [trans_taps, dw_kernels.reshape(layers * kernel, -1), ln_gain, ln_bias, w_out[None]], axis=0
    )
    small = jnp.concatenate([small, voiced_swap(small)], axis=1)
    router_share = other_half(w_router, 0)
    keep = jnp.where(lax.axis_index("rows") == 0, 0.0, 1.0).astype(F32).reshape(1, 1)

    turned = expert_ids.transpose(0, 2, 1)
    columns = slots * QUARTERS
    made = call(
        functools.partial(route_kernel, per_device),
        [
            shaped((rows, experts), F32),
            shaped((rows, columns), BF16),
            shaped((columns, QUARTERS * rows), BF16),
        ]
        * steps
        + [shaped((experts, columns), BF16)],
        offset.reshape(1, 1),
        jnp.concatenate([turned] * QUARTERS, axis=2),
        grant=16,
        flops=4 * steps * columns * experts * QUARTERS * rows,
    )
    spread = made[-1]
    hots, masks, picks = made[:-1:3], made[1:-1:3], made[2:-1:3]
    gate2 = up2 = down2 = router = None
    frames = None
    voiced = []

    def voice(frames):
        return call(
            functools.partial(vocoder_kernel, layers, kernel),
            shaped((rows, 2), F32),
            keep,
            frames,
            small,
            scratch=[
                pltpu.VMEM((2, rows + BACK, channels), F32),
                pltpu.VMEM((2, rows + BACK, channels), F32),
            ],
            flops=20 * rows * channels * kernel,
        )

    for step in range(steps):
        hot, mask, pick = hots[step], masks[step], picks[step]
        outgoing, normed = call(
            functools.partial(norm_kernel, depth),
            (HBM((slots * QUARTERS, width), BF16), HBM((QUARTERS * rows, width), BF16)),
            x,
            gain,
            pick,
            scratch=[
                pltpu.VMEM((QUARTERS * rows, width), BF16),
                pltpu.VMEM((QUARTERS, slots, width), BF16),
                pltpu.SemaphoreType.DMA((QUARTERS + 1,)),
            ],
            flops=2 * slots * QUARTERS * QUARTERS * rows * width,
        )
        received = lax.all_to_all(
            outgoing.reshape(experts, per_device * QUARTERS, width),
            "rows",
            split_axis=0,
            concat_axis=0,
            tiled=True,
        )
        if step == 0:
            gate2, up2, down2 = joined(gate_share, 0), joined(up_share, 0), joined(down_share, 0)
            router = ordered(w_router, joined(router_share, 0), 0)
        weights = call(
            weight_kernel,
            shaped((2 * rows, slots * QUARTERS), BF16),
            normed,
            router,
            hot,
            spread,
            mask,
            flops=4 * rows * experts * (depth + slots * QUARTERS),
        )
        if frames is not None:
            received, frames, weights = lax.optimization_barrier((received, frames, weights))
        answer = call(
            expert_kernel,
            HBM((slots * QUARTERS, width), BF16),
            received.reshape(slots * QUARTERS, width),
            gate,
            gate2,
            up,
            up2,
            down,
            down2,
            scratch=[
                pltpu.VMEM((width // LANES, slots * QUARTERS, LANES), F32),
                pltpu.VMEM((QUARTERS, slots, width), BF16),
                pltpu.SemaphoreType.DMA((QUARTERS,)),
            ],
            grant=12,
            flops=12 * slots * depth * w_gate.shape[2],
        )
        back = lax.all_to_all(
            answer.reshape(experts, per_device * QUARTERS, width),
            "rows",
            split_axis=0,
            concat_axis=0,
            tiled=True,
        )
        if frames is not None:
            sound = voice(frames)
            back, sound = lax.optimization_barrier((back, sound))
            voiced.append(sound)
        partial = call(
            combine_kernel,
            shaped((QUARTERS * rows, width), BF16),
            weights,
            back.reshape(slots * QUARTERS, width),
            flops=4 * slots * QUARTERS * QUARTERS * rows * width,
        )
        chip = lax.all_gather(partial, "segment", axis=0)
        chip = lax.dynamic_slice_in_dim(chip, seg * share, share, 1).astype(F32)
        chip = (chip[0] + chip[1]).astype(BF16)
        total = lax.all_gather(chip, "mp", axis=0).astype(F32)
        mine = lax.dynamic_slice_in_dim(x, seg * share, share, 0).astype(F32)
        fresh = (mine + (total[0] + total[1])).astype(BF16)
        x = lax.all_gather(fresh, "segment", axis=0, tiled=True)

        own = sum(
            dot(x[q * rows : (q + 1) * rows], w_in[q * width : (q + 1) * width])
            for q in range(QUARTERS)
        ).astype(BF16)
        last = own[-BACK:]
        near = jnp.concatenate([voiced_pass(last, 0), own], axis=0)
        far = jnp.concatenate([voiced_pass(last, 1), voiced_swap(own)], axis=0)
        frames = jnp.concatenate([near, far], axis=1)
    voiced.append(voice(frames))
    audio = jnp.stack([v.reshape(2 * rows) for v in voiced], axis=0)
    audio = jnp.where(seg == 0, jnp.zeros_like(audio), audio)[None]
    state = lax.dynamic_slice_in_dim(x, mp * share, share, 0)
    state = jnp.concatenate([state[:rows], state[rows:]], axis=1)
    return state, audio


def solution(mesh):
    return jax.shard_map(
        on_device,
        mesh=mesh,
        in_specs=(
            P("rows", "mp"),
            P(None, "rows", None),
            P("mp"),
            P("mp", None),
            P("rows", None, "mp"),
            P("rows", None, "mp"),
            P("rows", "mp", None),
            P(None, "mp"),
            P(None, "mp"),
            P(None, None, "mp"),
            P(None, "mp"),
            P(None, "mp"),
            P("mp"),
        ),
        out_specs=(P("rows", "mp"), P("segment", None, "rows")),
        check_vma=False,
    )
```

```python
import functools
import math

import jax
import jax.numpy as jnp
from jax import lax
from jax.experimental import pallas as pl
from jax.experimental.pallas import tpu as pltpu
from jax.sharding import PartitionSpec as P

BF16 = jnp.bfloat16
F32 = jnp.float32
QUARTERS = 4
BACK = 16
LANES = 128
VMEM = pltpu.VMEM
SMEM = pltpu.SMEM
HBM = pltpu.HBM


def dot(a, b):
    return jnp.dot(a, b, preferred_element_type=F32)


def dot_t(a, b):
    return lax.dot_general(a, b, (((1,), (1,)), ((), ())), preferred_element_type=F32)


def swapped(block, axis):
    return lax.ppermute(block, axis, [(0, 1), (1, 0)])


def voiced_swap(block):
    return lax.ppermute(block, ("segment", "mp"), [(2, 3), (3, 2)])


def voiced_pass(block, across):
    count = lax.axis_size("rows")
    route = [
        (2 * (count + i) + m, 2 * (count + i + 1) + (m ^ across))
        for i in range(count - 1)
        for m in range(2)
    ]
    return lax.ppermute(block, ("segment", "rows", "mp"), route)


def call(kernel, outs, *args, scratch=(), flops=0, places=None, grant=10):
    single = not isinstance(outs, (list, tuple))
    listed = [outs] if single else list(outs)
    moved = sum(math.prod(a.shape) * a.dtype.itemsize for a in list(args) + listed)
    places = places or [VMEM] * len(args)
    specs = [p if isinstance(p, pl.BlockSpec) else pl.BlockSpec(memory_space=p) for p in places]
    out_specs = [pl.BlockSpec(memory_space=getattr(o, "memory_space", VMEM)) for o in listed]
    out_specs = [
        s if s.memory_space in (VMEM, HBM) else pl.BlockSpec(memory_space=VMEM) for s in out_specs
    ]
    return pl.pallas_call(
        kernel,
        out_shape=outs,
        in_specs=specs,
        out_specs=out_specs[0] if single else out_specs,
        scratch_shapes=list(scratch),
        compiler_params=pltpu.CompilerParams(vmem_limit_bytes=grant * 1024 * 1024),
        cost_estimate=pl.CostEstimate(flops=flops, bytes_accessed=moved, transcendentals=0),
    )(*args)


def shaped(shape, dtype):
    return jax.ShapeDtypeStruct(shape, dtype)


def pack_kernel(
    seg_ref,
    state_ref,
    gain_ref,
    gate_ref,
    up_ref,
    down_ref,
    out_ref,
    head_out,
    head_ref,
    part_ref,
    sems,
):
    rows, half = state_ref.shape
    top = rows // 2
    share = gate_ref.shape[0] // 2
    from_row = pl.multiple_of(seg_ref[0, 0] * share, share)
    loads = []
    for i, ref in enumerate((gate_ref, up_ref, down_ref)):
        load = pltpu.make_async_copy(
            ref.at[pl.ds(from_row, share), :], part_ref.at[i], sems.at[i]
        )
        load.start()
        loads.append(load)
    head_ref[:top, :half] = state_ref[:top, :]
    head_ref[:top, half:] = state_ref[top:, :]
    gain = gain_ref[...]
    high = gain.astype(BF16)
    rest = gain - high.astype(F32)
    middle = rest.astype(BF16)
    low = (rest - middle.astype(F32)).astype(BF16)
    row = lax.broadcasted_iota(jnp.int32, (BACK, half), 0)
    terms = jnp.zeros((BACK, half), F32)
    for i, term in enumerate((high, middle, low)):
        terms = jnp.where(row == i, term.astype(F32), terms)
    head_ref[top:, :half] = terms.astype(BF16)
    head_ref[top:, half:] = terms.astype(BF16)
    copies = [
        pltpu.make_async_copy(head_ref, head_out, sems.at[3]),
    ]
    for copy in copies:
        copy.start()
    for i, load in enumerate(loads):
        load.wait()
        copy = pltpu.make_async_copy(
            part_ref.at[i], out_ref.at[pl.ds(i * share, share), :], sems.at[4 + i]
        )
        copy.start()
        copies.append(copy)
    for copy in copies:
        copy.wait()


def unpack_kernel(mp_ref, mine_ref, other_ref, x_ref, gain_ref):
    rows = x_ref.shape[0] // QUARTERS
    width = x_ref.shape[1]
    top = rows // 2
    ours = mp_ref[0, 0]
    for h in range(2):
        for q in range(2):
            for r in range(2):
                columns = slice((2 * r + q) * width, (2 * r + q + 1) * width)
                start = (2 * h + q) * rows + r * top
                mine = mine_ref[:top, columns].astype(F32)
                other = other_ref[:top, columns].astype(F32)
                x_ref[start : start + top, :] = jnp.where(ours == h, mine, other).astype(BF16)
            columns = slice(q * width, (q + 1) * width)
            mine = mine_ref[top : top + BACK, columns].astype(F32)
            other = other_ref[top : top + BACK, columns].astype(F32)
            terms = jnp.where(ours == h, mine, other)
            gain_ref[2 * h + q : 2 * h + q + 1, :] = (terms[0:1] + terms[1:2]) + terms[2:3]


def norm_kernel(
    depth, x_ref, gain_ref, pick_ref, out_ref, normed_out, x_out, normed_ref, held_ref, sems
):
    rows = x_ref.shape[0] // QUARTERS
    keep = pltpu.make_async_copy(x_ref, x_out, sems.at[QUARTERS + 1])
    keep.start()
    total = jnp.zeros((rows, 1), F32)
    for q in range(QUARTERS):
        part = x_ref[q * rows : (q + 1) * rows, :].astype(F32)
        total = total + jnp.sum(part * part, axis=1, keepdims=True)
    scale = lax.rsqrt(total / depth + 1e-06)
    for q in range(QUARTERS):
        part = x_ref[q * rows : (q + 1) * rows, :].astype(F32)
        normed_ref[q * rows : (q + 1) * rows, :] = (
            part * scale * gain_ref[q : q + 1, :]
        ).astype(BF16)
    copies = [keep, pltpu.make_async_copy(normed_ref, normed_out, sems.at[QUARTERS])]
    copies[1].start()
    normed = normed_ref[...]
    size = pick_ref.shape[0] // QUARTERS
    for i in range(QUARTERS):
        held_ref[i] = dot(pick_ref[i * size : (i + 1) * size, :], normed).astype(BF16)
        copy = pltpu.make_async_copy(
            held_ref.at[i], out_ref.at[pl.ds(i * size, size), :], sems.at[i]
        )
        copy.start()
        copies.append(copy)
    for copy in copies:
        copy.wait()


def weight_kernel(normed_ref, router_ref, hot_ref, spread_ref, mask_ref, out_ref):
    rows = normed_ref.shape[0] // QUARTERS
    width = normed_ref.shape[1]
    logits = jnp.zeros(hot_ref.shape, F32)
    for q in range(QUARTERS):
        logits = logits + dot(
            normed_ref[q * rows : (q + 1) * rows, :], router_ref[q * width : (q + 1) * width, :]
        )
    squashed = jnp.where(hot_ref[...] > 0.0, jax.nn.sigmoid(logits), 0.0)
    weights = squashed / jnp.sum(squashed, axis=1, keepdims=True)
    high = weights.astype(BF16)
    low = (weights - high.astype(F32)).astype(BF16)
    mask = mask_ref[...].astype(F32)
    out_ref[:rows, :] = (dot(high, spread_ref[...]) * mask).astype(BF16)
    out_ref[rows:, :] = (dot(low, spread_ref[...]) * mask).astype(BF16)


def expert_kernel(
    in_ref,
    gate_ref,
    gate2_ref,
    up_ref,
    up2_ref,
    down_ref,
    down2_ref,
    out_ref,
    wide_ref,
    answer_ref,
    sems,
):
    count, width = in_ref.shape
    slots = count // QUARTERS
    lanes = gate_ref.shape[0]
    pieces = width // LANES
    for c in range(pieces):
        wide_ref[c] = in_ref[:, c * LANES : (c + 1) * LANES].astype(F32)
    sums = [jnp.zeros((slots, lanes), F32) for _ in range(4)]
    for q in range(QUARTERS):
        part = jnp.concatenate(
            [wide_ref[c, pl.ds(q, slots, stride=QUARTERS), :] for c in range(pieces)], axis=1
        ).astype(BF16)
        columns = slice(q * width, (q + 1) * width)
        for i, ref in enumerate((gate_ref, gate2_ref, up_ref, up2_ref)):
            sums[i] = sums[i] + dot_t(part, ref[:, columns])
    first = (sums[0] / (1.0 + jnp.exp(-sums[0])) * sums[2]).astype(BF16)
    second = (sums[1] / (1.0 + jnp.exp(-sums[1])) * sums[3]).astype(BF16)
    for q in range(QUARTERS):
        columns = slice(q * width, (q + 1) * width)
        answer = dot(first, down_ref[:, columns]) + dot(second, down2_ref[:, columns])
        for c in range(pieces):
            wide_ref[c, pl.ds(q, slots, stride=QUARTERS), :] = answer[:, c * LANES : (c + 1) * LANES]
    stores = []
    size = count // QUARTERS
    for i in range(QUARTERS):
        span = slice(i * size, (i + 1) * size)
        for c in range(pieces):
            answer_ref[i, :, c * LANES : (c + 1) * LANES] = wide_ref[c, span, :].astype(BF16)
        store = pltpu.make_async_copy(
            answer_ref.at[i], out_ref.at[pl.ds(i * size, size), :], sems.at[i]
        )
        store.start()
        stores.append(store)
    for store in stores:
        store.wait()


def combine_kernel(weight_ref, back_ref, out_ref):
    rows = weight_ref.shape[0] // 2
    weights = weight_ref[...].astype(F32)
    lane = lax.broadcasted_iota(jnp.int32, weights.shape, 1) % QUARTERS
    chosen = jnp.concatenate(
        [jnp.where(lane == q, weights, 0.0).astype(BF16) for q in range(QUARTERS)], axis=0
    )
    mixed = dot(chosen, back_ref[...])
    for q in range(QUARTERS):
        start = 2 * q * rows
        out_ref[q * rows : (q + 1) * rows, :] = (
            mixed[start : start + rows] + mixed[start + rows : start + 2 * rows]
        ).astype(BF16)


def vocoder_kernel(layers, kernel, keep_ref, frame_ref, small_ref, out_ref, phase_ref, mixed_ref):
    count, channels = frame_ref.shape
    chunk = 256
    gains = 4 + layers * kernel
    blocks = [slice(c, c + chunk) for c in range(0, channels, chunk)]

    def back(value, frames):
        return value if frames == 0 else pltpu.roll(value, frames, 0)

    row = lax.broadcasted_iota(jnp.int32, (count, 1), 0)
    live = jnp.where(row < BACK, keep_ref[0, 0], 1.0)
    for block in blocks:
        now = frame_ref[:, block].astype(F32)
        before = back(now, 1)
        for p in range(2):
            phase_ref[p, :, block] = (
                small_ref[p : p + 1, block] * now + small_ref[p + 2 : p + 3, block] * before
            ).astype(BF16).astype(F32)
    for i in range(layers):
        dilation = 3**i
        sums = [jnp.zeros((count, 1), F32) for _ in range(2)]
        powers = [jnp.zeros((count, 1), F32) for _ in range(2)]
        for block in blocks:
            phases = [phase_ref[0, :, block], phase_ref[1, :, block]]
            for p in range(2):
                mixed = jnp.zeros((count, chunk), F32)
                for j in range(kernel):
                    at = p - j * dilation
                    tap = small_ref[4 + i * kernel + j : 5 + i * kernel + j, block]
                    mixed = mixed + tap * back(phases[at % 2], -(at // 2))
                mixed_ref[p, :, block] = mixed
                sums[p] = sums[p] + jnp.sum(mixed, axis=1, keepdims=True)
                powers[p] = powers[p] + jnp.sum(mixed * mixed, axis=1, keepdims=True)
        for p in range(2):
            center = sums[p] / channels
            scale = lax.rsqrt(powers[p] / channels - center * center + 1e-06)
            voice = jnp.zeros((count, 1), F32)
            for block in blocks:
                gain = small_ref[gains + i : gains + i + 1, block]
                bias = small_ref[gains + layers + i : gains + layers + i + 1, block]
                fresh = (
                    phase_ref[p, :, block]
                    + (mixed_ref[p, :, block] - center) * scale * gain
                    + bias
                )
                fresh = fresh.astype(BF16).astype(F32)
                if i < layers - 1:
                    phase_ref[p, :, block] = fresh * live
                else:
                    wave = small_ref[gains + 2 * layers : gains + 2 * layers + 1, block]
                    voice = voice + jnp.sum(fresh * wave, axis=1, keepdims=True)
            if i == layers - 1:
                out_ref[:, p : p + 1] = voice[BACK:, :]


def other_half(weight, axis):
    seg = lax.axis_index("segment")
    share = weight.shape[axis] // 2
    mine = lax.dynamic_slice_in_dim(weight, seg * share, share, axis)
    return swapped(mine, "mp")


def joined(share, axis):
    return lax.all_gather(share, "segment", axis=axis, tiled=True)


def route_kernel(per_device, offset_ref, ids_ref, *out_refs):
    steps, topk, wide = ids_ref.shape
    rows = wide // QUARTERS
    spread_ref = out_refs[-1]
    experts, columns = spread_ref.shape
    group = per_device * QUARTERS

    def iota(shape, axis):
        return lax.broadcasted_iota(jnp.int32, shape, axis)

    def ones(condition):
        return jnp.where(condition, 1.0, 0.0)

    name = iota((experts, wide), 0)
    ahead, behind = iota((wide, wide), 0), iota((wide, wide), 1)
    same = ahead // rows == behind // rows
    below = ones(same & (ahead % rows < behind % rows)).astype(BF16)
    unit = ones(iota((rows, wide), 0) == iota((rows, wide), 1)).astype(BF16)
    spread = ones(iota((experts, columns), 1) // group == iota((experts, columns), 0)).astype(BF16)
    tall = ones(iota((columns, experts), 0) // group == iota((columns, experts), 1)).astype(BF16)
    slot_row = iota((1, columns), 1) // QUARTERS % per_device
    column = iota((columns, wide), 0)
    slot_column = (column // QUARTERS % per_device).astype(F32)
    own = column % QUARTERS == iota((columns, wide), 1) // rows
    spread_ref[...] = spread
    for s in range(steps):
        hot_ref, mask_ref, pick_ref = out_refs[3 * s : 3 * s + 3]
        named = jnp.zeros((experts, wide), F32)
        for k in range(topk):
            named = named + ones(ids_ref[s, k : k + 1, :] == name)
        earlier = dot(named.astype(BF16), below)
        code = jnp.where(named > 0.0, earlier - offset_ref[0, 0], -64.0).astype(BF16)
        upright = dot_t(unit, code)
        hot_ref[...] = ones(upright > -32.0)
        mask_ref[...] = ones(dot(upright.astype(BF16), spread) == slot_row.astype(F32)).astype(BF16)
        pick_ref[...] = ones((dot(tall, code) == slot_column) & own).astype(BF16)


def on_device(
    start_state,
    expert_ids,
    norm_gain,
    w_router,
    w_gate,
    w_up,
    w_down,
    w_in,
    trans_taps,
    dw_kernels,
    ln_gain,
    ln_bias,
    w_out,
):
    seg = lax.axis_index("segment")
    mp = lax.axis_index("mp")
    rows, half = start_state.shape
    experts = w_router.shape[1]
    steps, _, topk = expert_ids.shape
    layers, kernel, channels = dw_kernels.shape
    channels = 2 * channels
    capacity = min(rows, max(2, 2 * rows * topk // experts))
    per_device = capacity // 4
    slots = experts * per_device
    offset = ((mp * 2 + seg) * per_device).astype(F32)
    depth = 2 * half
    width = depth // QUARTERS
    share = 2 * rows

    def ordered(mine, other, axis):
        return jnp.where(
            mp == 0,
            jnp.concatenate([mine, other], axis=axis),
            jnp.concatenate([other, mine], axis=axis),
        )

    gate, up, down = w_gate[0].T, w_up[0].T, w_down[0]
    part = gate.shape[0] // 2
    top = rows // 2
    packed, head = call(
        pack_kernel,
        (HBM((3 * part, depth), BF16), HBM((top + BACK, depth), BF16)),
        seg.astype(jnp.int32).reshape(1, 1),
        start_state,
        norm_gain[None],
        gate,
        up,
        down,
        scratch=[
            pltpu.VMEM((top + BACK, depth), BF16),
            pltpu.VMEM((3, part, depth), BF16),
            pltpu.SemaphoreType.DMA((7,)),
        ],
        places=[SMEM, VMEM, VMEM, HBM, HBM, HBM],
        grant=60,
    )
    head_sent = swapped(head, "mp")
    sent = swapped(packed, "mp")
    x, gain = call(
        unpack_kernel,
        (shaped((QUARTERS * rows, width), BF16), shaped((QUARTERS, width), F32)),
        mp.astype(jnp.int32).reshape(1, 1),
        head,
        head_sent,
        places=[SMEM, VMEM, VMEM],
    )
    gate_share, up_share, down_share = (
        sent[i * part : (i + 1) * part] for i in range(3)
    )
    small = jnp.concatenate(
        [trans_taps, dw_kernels.reshape(layers * kernel, -1), ln_gain, ln_bias, w_out[None]], axis=0
    )
    small = jnp.concatenate([small, voiced_swap(small)], axis=1)
    router_share = other_half(w_router, 0)
    keep = jnp.where(lax.axis_index("rows") == 0, 0.0, 1.0).astype(F32).reshape(1, 1)

    turned = expert_ids.transpose(0, 2, 1)
    columns = slots * QUARTERS
    made = call(
        functools.partial(route_kernel, per_device),
        [
            shaped((rows, experts), F32),
            shaped((rows, columns), BF16),
            shaped((columns, QUARTERS * rows), BF16),
        ]
        * steps
        + [shaped((experts, columns), BF16)],
        offset.reshape(1, 1),
        jnp.concatenate([turned] * QUARTERS, axis=2),
        grant=16,
        flops=4 * steps * columns * experts * QUARTERS * rows,
    )
    spread = made[-1]
    hots, masks, picks = made[:-1:3], made[1:-1:3], made[2:-1:3]
    gate2 = up2 = down2 = router = None
    frames = None
    voiced = []

    def rendered_frames(x):
        own = sum(
            dot(x[q * rows : (q + 1) * rows], w_in[q * width : (q + 1) * width])
            for q in range(QUARTERS)
        ).astype(BF16)
        last = own[-BACK:]
        near = jnp.concatenate([voiced_pass(last, 0), own], axis=0)
        far = jnp.concatenate([voiced_pass(last, 1), voiced_swap(own)], axis=0)
        return jnp.concatenate([near, far], axis=1)

    def voice(frames):
        return call(
            functools.partial(vocoder_kernel, layers, kernel),
            shaped((rows, 2), F32),
            keep,
            frames,
            small,
            scratch=[
                pltpu.VMEM((2, rows + BACK, channels), F32),
                pltpu.VMEM((2, rows + BACK, channels), F32),
            ],
            flops=20 * rows * channels * kernel,
        )

    for step in range(steps):
        hot, mask, pick = hots[step], masks[step], picks[step]
        outgoing, normed, x = call(
            functools.partial(norm_kernel, depth),
            (
                HBM((slots * QUARTERS, width), BF16),
                HBM((QUARTERS * rows, width), BF16),
                HBM((QUARTERS * rows, width), BF16),
            ),
            x,
            gain,
            pick,
            scratch=[
                pltpu.VMEM((QUARTERS * rows, width), BF16),
                pltpu.VMEM((QUARTERS, slots, width), BF16),
                pltpu.SemaphoreType.DMA((QUARTERS + 2,)),
            ],
            flops=2 * slots * QUARTERS * QUARTERS * rows * width,
        )
        if step > 0:
            frames = rendered_frames(x)
        received = lax.all_to_all(
            outgoing.reshape(experts, per_device * QUARTERS, width),
            "rows",
            split_axis=0,
            concat_axis=0,
            tiled=True,
        )
        if step == 0:
            gate2, up2, down2 = joined(gate_share, 0), joined(up_share, 0), joined(down_share, 0)
            router = ordered(w_router, joined(router_share, 0), 0)
        weights = call(
            weight_kernel,
            shaped((2 * rows, slots * QUARTERS), BF16),
            normed,
            router,
            hot,
            spread,
            mask,
            flops=4 * rows * experts * (depth + slots * QUARTERS),
        )
        if frames is not None:
            received, frames, weights = lax.optimization_barrier((received, frames, weights))
        answer = call(
            expert_kernel,
            HBM((slots * QUARTERS, width), BF16),
            received.reshape(slots * QUARTERS, width),
            gate,
            gate2,
            up,
            up2,
            down,
            down2,
            scratch=[
                pltpu.VMEM((width // LANES, slots * QUARTERS, LANES), F32),
                pltpu.VMEM((QUARTERS, slots, width), BF16),
                pltpu.SemaphoreType.DMA((QUARTERS,)),
            ],
            grant=12,
            flops=12 * slots * depth * w_gate.shape[2],
        )
        back = lax.all_to_all(
            answer.reshape(experts, per_device * QUARTERS, width),
            "rows",
            split_axis=0,
            concat_axis=0,
            tiled=True,
        )
        if frames is not None:
            sound = voice(frames)
            back, sound = lax.optimization_barrier((back, sound))
            voiced.append(sound)
        partial = call(
            combine_kernel,
            shaped((QUARTERS * rows, width), BF16),
            weights,
            back.reshape(slots * QUARTERS, width),
            flops=4 * slots * QUARTERS * QUARTERS * rows * width,
        )
        chip = lax.all_gather(partial, "segment", axis=0)
        chip = lax.dynamic_slice_in_dim(chip, seg * share, share, 1).astype(F32)
        chip = (chip[0] + chip[1]).astype(BF16)
        total = lax.all_gather(chip, "mp", axis=0).astype(F32)
        mine = lax.dynamic_slice_in_dim(x, seg * share, share, 0).astype(F32)
        fresh = (mine + (total[0] + total[1])).astype(BF16)
        x = lax.all_gather(fresh, "segment", axis=0, tiled=True)

    frames = rendered_frames(x)
    voiced.append(voice(frames))
    audio = jnp.stack([v.reshape(2 * rows) for v in voiced], axis=0)
    audio = jnp.where(seg == 0, jnp.zeros_like(audio), audio)[None]
    state = lax.dynamic_slice_in_dim(x, mp * share, share, 0)
    state = jnp.concatenate([state[:rows], state[rows:]], axis=1)
    return state, audio


def solution(mesh):
    return jax.shard_map(
        on_device,
        mesh=mesh,
        in_specs=(
            P("rows", "mp"),
            P(None, "rows", None),
            P("mp"),
            P("mp", None),
            P("rows", None, "mp"),
            P("rows", None, "mp"),
            P("rows", "mp", None),
            P(None, "mp"),
            P(None, "mp"),
            P(None, None, "mp"),
            P(None, "mp"),
            P(None, "mp"),
            P("mp"),
        ),
        out_specs=(P("rows", "mp"), P("segment", None, "rows")),
        check_vma=False,
    )
```
